768 devices in a mesh: gx: 96 (over y, z), gy: 8 (over x, core).
Axes of the slice: x: 4, y: 8, z: 12, core: 2. Of those that a mesh axis runs over, the one named last changes fastest.
Arguments:
- multipoles: bfloat16 [49152, 256], P(('gx', 'gy')), may hold values from -4 to 4
- operators: bfloat16 [16, 256, 256], replicated, may hold values from -0.375 to 0.375
- pairs: int32 [3, 786432], P(None, ('gx', 'gy')), may hold values from 0 to 687, as said below
- pair_count: int32 [768], P(('gx', 'gy')), may hold values from 256 to 1024, as said below
- send_list: int32 [479232], P(('gx', 'gy')), may hold values from 0 to 63
Outputs:
- local_field: float32 [49152, 256], P(('gx', 'gy'))
The draws below stay inside these ranges and needn't reach their ends.
Inputs may be any that keep to these rules, and one draw needn't show every extreme that they name: `pairs`: A source index below 64 is the device's own box; a larger one names slot (u - 64) % 24 of neighbour lane (u - 64) // 24, and the block in that direction lies on the grid. Targets are below 64, operators below 16. `pair_count`: some device uses all 1024 slots.
All inputs are finite; a program needn't handle non-finite values.
Results may differ from the reference program's by a relative error of at most 0.00035.
Values may be sent and summed in bfloat16 or wider, within the bound.
A program may use at most 64 MiB of HBM per device.

```python
import jax
import jax.numpy as jnp
from jax import lax

POINTS = 256
OPERATORS = 16
LANES = 26
BOXES = 64
PAIRS = 1024
SLOTS = 24
NBY = 8
BOX_TOTAL = 49152
N_GX = 96
N_GY = 8
DEVICES = 768


def draw_pairs(key, part):
    key = jax.random.fold_in(key, 7)
    key_kind, key_slot, key_own, key_target, key_operator = jax.random.split(key, 5)
    total = DEVICES * PAIRS
    device = jnp.arange(total, dtype=jnp.int32) // PAIRS
    kind_draw = jax.random.randint(key_kind, (total,), 0, 3)
    slot_draw = jax.random.randint(key_slot, (total,), 0, LANES * SLOTS)
    lane_index = slot_draw // SLOTS
    lane_code = jnp.where(lane_index < 13, lane_index, lane_index + 1)
    outer = device // N_GY
    next_x = device % N_GY + lane_code // 9 - 1
    next_y = outer % NBY + lane_code // 3 % 3 - 1
    next_z = outer // NBY + lane_code % 3 - 1
    on_grid = (next_x >= 0) & (next_x < N_GY) & (next_y >= 0) & (next_y < NBY) & (next_z >= 0) & (next_z < N_GX // NBY)
    usable = (kind_draw > 0) & on_grid
    own_draw = jax.random.randint(key_own, (total,), 0, BOXES)
    source_ids = jnp.where(usable, BOXES + slot_draw, own_draw)
    target_ids = jax.random.randint(key_target, (total,), 0, BOXES)
    operator_ids = jax.random.randint(key_operator, (total,), 0, OPERATORS)
    return jnp.stack([source_ids, target_ids, operator_ids]).astype(jnp.int32)


def draw_pair_count(key, part):
    key = jax.random.fold_in(key, 9)
    key_level, key_busiest = jax.random.split(key, 2)
    level = jax.random.randint(key_level, (DEVICES,), 0, 3)
    counts = jnp.right_shift(jnp.full((DEVICES,), PAIRS, jnp.int32), level.astype(jnp.int32))
    busiest = jax.random.randint(key_busiest, (), 0, DEVICES)
    return counts.at[busiest].set(PAIRS).astype(jnp.int32)


def plant(entries, own_key, least, largest):
    place = [jax.random.randint(jax.random.fold_in(own_key, axis), (), 0, length) for axis, length in enumerate(entries.shape)]
    longest = entries.shape.index(max(entries.shape))
    beside = place[:longest] + [(place[longest] + 1) % entries.shape[longest]] + place[longest + 1:]
    return entries.at[tuple(place)].set(least).at[tuple(beside)].set(largest)


def level_of(key, dims, pieces, smallest, high):
    def one(dim, parts):
        heights = jax.random.uniform(jax.random.fold_in(jax.random.fold_in(key, 6), dim), (parts,), jnp.float32, smallest / len(pieces), high / len(pieces))
        return jnp.repeat(jnp.exp(heights), dims[dim] // parts).reshape((-1,) + (1,) * (len(dims) - dim - 1))

    loudness = one(*pieces[0])
    for cut in pieces[1:]:
        loudness = loudness * one(*cut)
    return loudness


def centred(key, extent, spread, limit, pieces=(), kind=jnp.bfloat16):
    level = level_of(key, extent, pieces, -0.22, 0.18) if pieces else 1.0
    array = jax.random.normal(key, extent, jnp.float32) * spread * level
    return jnp.minimum(jnp.maximum(array, -limit), limit).astype(kind)


def setup_inputs(seed: int = 0) -> dict:
    key_list = jax.random.split(jax.random.key(seed), 6)
    return {
        "multipoles": centred(key_list[0], (BOX_TOTAL, POINTS), 0.5, 4.0, ((0, 768),)),
        "operators": centred(key_list[1], (OPERATORS, POINTS, POINTS), POINTS ** -0.5, 0.375),
        "pairs": draw_pairs(jax.random.fold_in(key_list[5], 71), 0),
        "pair_count": draw_pair_count(jax.random.fold_in(key_list[5], 71), 0),
        "send_list": plant(jax.random.randint(key_list[4], (DEVICES * LANES * SLOTS,), 0, BOXES), jax.random.fold_in(key_list[4], 1), 0, BOXES - 1).astype(jnp.int32),
    }


def reference(multipoles, operators, pairs, pair_count, send_list):
    total = DEVICES * PAIRS
    box_total = DEVICES * BOXES
    positions = jnp.arange(total, dtype=jnp.int32)
    device = positions // PAIRS
    in_use = (positions % PAIRS) < pair_count[device]
    source_ids = pairs[0]
    target_ids = pairs[1]
    operator_ids = pairs[2]
    is_ghost = source_ids >= BOXES
    slot_index = jnp.clip(source_ids - BOXES, 0, LANES * SLOTS - 1)
    lane_index = slot_index // SLOTS
    lane_code = jnp.where(lane_index < 13, lane_index, lane_index + 1)
    delta_x = lane_code // 9 - 1
    delta_y = (lane_code // 3) % 3 - 1
    delta_z = lane_code % 3 - 1
    outer = device // N_GY
    block_x = device % N_GY
    block_y = outer % NBY
    block_z = outer // NBY
    sender = ((block_z + delta_z) * NBY + (block_y + delta_y)) * N_GY + (block_x + delta_x)
    sender = jnp.clip(sender, 0, DEVICES - 1)
    sent_box = sender * BOXES + send_list[sender * (LANES * SLOTS) + slot_index]
    source_box = jnp.where(is_ghost, sent_box, device * BOXES + jnp.clip(source_ids, 0, BOXES - 1)).astype(jnp.int32)
    target_box = (device * BOXES + target_ids).astype(jnp.int32)

    def one_operator(field_sum, operator_index):
        matrix = operators[operator_index]
        outward = jnp.dot(multipoles, matrix, preferred_element_type=jnp.float32)
        mirrored = jnp.dot(multipoles, matrix.T, preferred_element_type=jnp.float32)
        chosen = (in_use & (operator_ids == operator_index))[:, None]
        field_sum = field_sum + jax.ops.segment_sum(jnp.where(chosen, outward[source_box], 0.0), target_box, box_total)
        field_sum = field_sum + jax.ops.segment_sum(jnp.where(chosen, mirrored[target_box], 0.0), source_box, box_total)
        return field_sum, None

    start = jnp.zeros((box_total, POINTS), jnp.float32)
    field_sum, unused = lax.scan(one_operator, start, jnp.arange(OPERATORS, dtype=jnp.int32))
    return field_sum
```

```python
import functools

import jax
import jax.numpy as jnp
from jax import lax
from jax.experimental import pallas as pl
from jax.experimental.pallas import tpu as pltpu
from jax.sharding import PartitionSpec as P

MESH = pl.DeviceIdType.MESH
F32 = jnp.float32
BF16 = jnp.bfloat16
I32 = jnp.int32

BOXES = 64
POINTS = 256
PAIRS = 1024
LANES = 26
SLOTS = 24
OPS = 16
OWN = 13
ROWS = 80
WINDOW = 64


def code_of(lane):
    return lane if lane < OWN else lane + 1


def heading(code):
    return code // 9 - 1, code // 3 % 3 - 1, code % 3 - 1


def iota(shape, axis):
    return lax.broadcasted_iota(I32, shape, axis)


def one_hot(condition):
    return jnp.where(condition, 1.0, 0.0).astype(BF16)


def nt(a, b):
    return lax.dot_general(a, b, (((1,), (1,)), ((), ())), preferred_element_type=F32)


def mm(a, b):
    return jnp.dot(a, b, preferred_element_type=F32)


def pack_block(count, pairs_ref, send_ref, m_ref, block, meta):
    source = pairs_ref[0:1, :]
    target = pairs_ref[1:2, :]
    operator = pairs_ref[2:3, :]
    used = iota((1, PAIRS), 1) < count
    ghost = jnp.maximum(source - BOXES, 0)
    lane = jnp.right_shift(ghost * 2731, 16)
    slot = ghost - lane * SLOTS
    lane = jnp.where(used, jnp.where(source < BOXES, LANES, lane), 31)
    codes = iota((32, PAIRS), 0)
    start = jnp.sum(jnp.where(lane < codes, 1.0, 0.0), axis=1, keepdims=True)
    before = one_hot(iota((128, 128), 0) < iota((128, 128), 1))
    carry = start
    places = []
    for chunk in range(PAIRS // 128):
        hot = jnp.where(codes[:, :128] == lane[:, chunk * 128:(chunk + 1) * 128], 1.0, 0.0)
        rank = mm(hot.astype(BF16), before) + carry
        places.append(jnp.sum(hot * rank, axis=0, keepdims=True))
        carry = carry + jnp.sum(hot, axis=1, keepdims=True)
    place = jnp.concatenate(places, axis=1).astype(I32)
    fields = jnp.concatenate(
        [slot, target, operator, jnp.zeros((5, PAIRS), I32)], axis=0
    ).astype(F32).astype(BF16)
    for q in range(4):
        hot = one_hot(iota((256, PAIRS), 0) + 256 * q == place)
        ordered = nt(fields, hot)
        meta[4 * q:4 * q + 3, :] = ordered[0:3, :]
    sends = send_ref[...].astype(F32)
    for q in range(3):
        meta[4 * q + 3:4 * q + 4, :] = sends[:, 256 * q:256 * q + 256]
    diagonal = iota((32, 128), 0) == iota((32, 128), 1)
    starts = jnp.sum(jnp.where(diagonal, start, 0.0), axis=0, keepdims=True).astype(I32)
    high = jnp.right_shift(starts, 5)
    meta[15:16, 0:128] = high.astype(F32)
    meta[15:16, 128:256] = (starts - high * 32).astype(F32)
    block[0:BOXES, :] = m_ref[...]
    block[BOXES:ROWS, :] = meta[...].astype(BF16)


def exchange_kernel(nx, ny, nz, count_ref, pairs_ref, send_ref, m_ref, out_ref, meta, send_sem, recv_sem):
    g = lax.axis_index("gx")
    h = lax.axis_index("gy")
    by = lax.rem(g, ny)
    bz = lax.div(g, ny)
    steps = {
        "z": {1: bz < nz - 1, -1: bz > 0, 0: True},
        "y": {1: by < ny - 1, -1: by > 0, 0: True},
        "x": {1: h < nx - 1, -1: h > 0, 0: True},
    }
    partner = {
        "z": lambda s: (g + s * ny, h),
        "y": lambda s: (g + s, h),
        "x": lambda s: (g, h + s),
    }

    def on_grid(dx, dy, dz):
        cond = None
        for flag in (steps["x"][dx], steps["y"][dy], steps["z"][dz]):
            if flag is not True:
                cond = flag if cond is None else jnp.logical_and(cond, flag)
        return cond

    barrier = pltpu.get_barrier_semaphore()
    for axis in "zyx":
        for s in (1, -1):
            @pl.when(steps[axis][s])
            def _():
                pl.semaphore_signal(barrier, inc=1, device_id=partner[axis](s), device_id_type=MESH)

    pack_block(count_ref[0], pairs_ref, send_ref, m_ref, out_ref.at[OWN], meta)

    for code in range(27):
        if code != OWN:
            @pl.when(jnp.logical_not(on_grid(*heading(code))))
            def _():
                out_ref[code] = jnp.zeros((ROWS, POINTS), BF16)

    pl.semaphore_wait(
        barrier,
        sum(steps[axis][s].astype(I32) for axis in "zyx" for s in (1, -1)),
    )

    def as_code(dx, dy, dz):
        return (dx + 1) * 9 + (dy + 1) * 3 + dz + 1

    started = []

    def send(src, axis, s):
        dx, dy, dz = src
        dst = {"x": (-s, dy, dz), "y": (dx, -s, dz), "z": (dx, dy, -s)}[axis]
        need = {"x": (s, dy, dz), "y": (dx, s, dz), "z": (dx, dy, s)}[axis]
        cond = on_grid(*need)
        copy = pltpu.make_async_remote_copy(
            src_ref=out_ref.at[as_code(*src)],
            dst_ref=out_ref.at[as_code(*dst)],
            send_sem=send_sem.at[len(started)],
            recv_sem=recv_sem.at[as_code(*dst)],
            device_id=partner[axis](s),
            device_id_type=MESH,
        )
        started.append((copy, cond))
        pl.when(cond)(copy.start)

    def arrived(where):
        code = as_code(*where)
        slot = out_ref.at[code]
        copy = pltpu.make_async_remote_copy(
            src_ref=slot, dst_ref=slot, send_sem=send_sem.at[0], recv_sem=recv_sem.at[code],
            device_id=(g, h), device_id_type=MESH,
        )
        pl.when(on_grid(*where))(copy.wait_recv)

    home = (0, 0, 0)
    for axis in "zyx":
        for s in (1, -1):
            send(home, axis, s)
    for where in [(0, 1, 0), (0, -1, 0)]:
        arrived(where)
        for s in (1, -1):
            send(where, "x", s)
    for where in [(0, 0, 1), (0, 0, -1)]:
        arrived(where)
        for axis in "yx":
            for s in (1, -1):
                send(where, axis, s)
    for where in [(0, 1, 1), (0, -1, 1), (0, 1, -1), (0, -1, -1)]:
        arrived(where)
        for s in (1, -1):
            send(where, "x", s)
    for code in range(27):
        if heading(code)[0] != 0:
            arrived(heading(code))
    for copy, cond in started:
        pl.when(cond)(copy.wait_send)


def column(row):
    n = row.shape[1]
    parts = []
    for c in range(n // 128):
        piece = jnp.broadcast_to(row[:, c * 128:(c + 1) * 128], (8, 128))
        parts.append(jnp.transpose(piece)[:, 0:1])
    return jnp.concatenate(parts, axis=0)


def compute_kernel(count_ref, pairs_ref, blocks, ops_ref, out_ref, meta, starts_v, starts_s, events, ghost, rows_f, rows_m, keys_m, zm, copy_sem):
    for code in range(27):
        wide = blocks[code, BOXES:ROWS, :].astype(F32)
        for q in range(4):
            meta[code, q, 0:4, :] = wide[4 * q:4 * q + 4, :]
            meta[code, q, 4:8, :] = wide[4 * q:4 * q + 4, :]
        starts_v[code:code + 1, :] = (wide[15:16, 0:128] * 32.0 + wide[15:16, 128:256]).astype(I32)
    copy = pltpu.make_async_copy(starts_v, starts_s, copy_sem)
    copy.start()

    source = pairs_ref[0:1, :]
    target = pairs_ref[1:2, :]
    operator = pairs_ref[2:3, :]
    used = iota((1, PAIRS), 1) < count_ref[0]
    key_f = jnp.where(used, operator * BOXES + target, -1)
    keys_m[0:1, 0:PAIRS] = jnp.where(
        jnp.logical_and(used, source < BOXES), operator * BOXES + source, -1
    )
    boxes = []
    for q in range(3):
        flat = iota((1, 256), 1) + 256 * q
        row = jnp.full((1, 256), -1.0, F32)
        for lane in range(LANES):
            low = lane * SLOTS
            if low < 256 * (q + 1) and low + SLOTS > 256 * q:
                mine = jnp.logical_and(flat >= low, flat < low + SLOTS)
                row = jnp.where(mine, meta[code_of(lane), q, 3:4, :], row)
        boxes.append(row)
    box_column = column(jnp.concatenate(boxes, axis=1)).astype(I32)
    own_boxes = column(
        jnp.concatenate([meta[OWN, q, 3:4, :] for q in range(3)], axis=1)
    )
    copy.wait()

    across = iota((8, 128), 1)

    def window(code, begin, offset):
        begin = jnp.minimum(begin, PAIRS - 1)
        chunk = lax.div(begin, 128)
        after = jnp.minimum(chunk + 1, 7)

        def piece(c):
            return meta[code, lax.div(c, 2), :, pl.ds(pl.multiple_of(lax.rem(c, 2) * 128, 128), 128)]

        shift = begin - chunk * 128
        turn = lax.rem(256 + offset - shift, 128)
        first = pltpu.roll(piece(chunk), turn, 1)
        second = pltpu.roll(piece(after), turn, 1)
        return jnp.where(across < 128 - shift + offset, first, second)

    def own_box(slots, lane_boxes):
        hot = iota((SLOTS, 128), 0) == slots.astype(I32)
        return jnp.sum(jnp.where(hot, lane_boxes, 0.0), axis=0, keepdims=True)

    def lane_span(code, back):
        begin = starts_s[code, back]
        return begin, starts_s[code, back + 1] - begin

    for pair in range(LANES // 2):
        halves = []
        for half in range(2):
            lane = 2 * pair + half
            code, back = code_of(lane), LANES - 1 - lane
            begin, count = lane_span(code, back)
            part = window(code, begin, 64 * half)
            box = own_box(part[0:1, :], own_boxes[back * SLOTS:(back + 1) * SLOTS, :])
            key = (part[2:3, :] * BOXES + box).astype(I32)
            key = jnp.where(across[0:1, :] - 64 * half < count, key, -1)
            halves.append((part, key))
        low = across < 64
        events[:, pair * 128:(pair + 1) * 128] = jnp.where(low, halves[0][0], halves[1][0])
        keys_m[0:1, PAIRS + pair * 128:PAIRS + (pair + 1) * 128] = jnp.where(
            low[0:1, :], halves[0][1], halves[1][1]
        )

    ghost[0:BOXES, :] = blocks[OWN, 0:BOXES, :]
    ghost[BOXES + LANES * SLOTS:, :] = jnp.zeros((768 - BOXES - LANES * SLOTS, POINTS), BF16)
    for group in range(7):
        lanes = list(range(4 * group, min(4 * group + 4, LANES)))
        width = 64 * len(lanes)
        base = group * 256
        table = jnp.concatenate([blocks[code_of(lane), 0:BOXES, :] for lane in lanes], axis=0)
        targets = column(events[1:2, base:base + width]).astype(I32)
        which = jnp.right_shift(iota((width, 1), 0), 6)
        hot = one_hot(iota((width, width), 1) == targets + 64 * which)
        rows_m[PAIRS + base:PAIRS + base + width, :] = mm(hot, table).astype(BF16)
        picks = []
        for i, lane in enumerate(lanes):
            picked = box_column[lane * SLOTS:(lane + 1) * SLOTS, :] + 64 * i
            picks.append(jnp.where(iota((SLOTS, width), 1) == picked, 1.0, 0.0))
        hot = jnp.concatenate(picks, axis=0).astype(BF16)
        first = BOXES + SLOTS * lanes[0]
        ghost[first:first + SLOTS * len(lanes), :] = mm(hot, table).astype(BF16)

    source_column = column(source.astype(F32)).astype(I32)
    target_column = column(target.astype(F32)).astype(I32)
    for q in range(4):
        span = slice(q * 256, (q + 1) * 256)
        hot = one_hot(iota((256, 768), 1) == source_column[span, :])
        rows_f[span, :] = mm(hot, ghost[...]).astype(BF16)
        hot = one_hot(iota((256, BOXES), 1) == target_column[span, :])
        rows_m[span, :] = mm(hot, blocks[OWN, 0:BOXES, :]).astype(BF16)

    width_m = PAIRS + LANES * 64

    zm[...] = jnp.zeros_like(zm)

    @pl.loop(0, LANES)
    def _(lane):
        code = jnp.where(lane < OWN, lane, lane + 1)
        back = LANES - 1 - lane
        begin, count = lane_span(code, back)

        @pl.loop(1, lax.div(count + WINDOW - 1, WINDOW))
        def _(turn):
            part = window(code, begin + turn * WINDOW, 0)
            flat = iota((1, 128), 1)
            boxes_row = jnp.zeros((1, 128), F32)
            slots = part[0:1, :].astype(I32) + back * SLOTS
            for q in range(6):
                spread = own_boxes[q * 128:(q + 1) * 128, :]
                hot = iota((128, 128), 0) + 128 * q == slots
                boxes_row += jnp.sum(jnp.where(hot, spread, 0.0), axis=0, keepdims=True)
            key = (part[2:3, :] * BOXES + boxes_row).astype(I32)
            left = jnp.minimum(count - turn * WINDOW, WINDOW)
            key = jnp.where(flat < left, key, -1)
            hot = one_hot(iota((128, BOXES), 1) == column(part[1:2, :]).astype(I32))
            rows = mm(hot, blocks[code, 0:BOXES, :]).astype(BF16)
            for q in range(4):
                hot = one_hot(iota((256, 128), 0) + 256 * q == key)
                zm[256 * q:256 * (q + 1), :] += mm(hot, rows)

    total = jnp.zeros((128, POINTS), F32)
    for q in range(4):
        hot = one_hot(iota((256, PAIRS), 0) + 256 * q == key_f)
        forward = mm(hot, rows_f[...])
        hot = one_hot(iota((256, width_m), 0) + 256 * q == keys_m[...])
        mirror = mm(hot, rows_m[...]) + zm[256 * q:256 * (q + 1), :]
        f_high = forward.astype(BF16)
        f_low = (forward - f_high.astype(F32)).astype(BF16)
        m_high = mirror.astype(BF16)
        m_low = (mirror - m_high.astype(F32)).astype(BF16)
        for i in range(4):
            part = slice(64 * i, 64 * i + 64)
            matrix = ops_ref[4 * q + i]
            total += mm(jnp.concatenate([f_high[part], f_low[part]], axis=0), matrix)
            total += nt(jnp.concatenate([m_high[part], m_low[part]], axis=0), matrix)
    out_ref[...] = total[0:BOXES, :] + total[BOXES:, :]


def local(sizes, multipoles, operators, pairs, pair_count, send_list):
    nx, ny, nz = sizes
    vmem = pl.BlockSpec(memory_space=pltpu.VMEM)
    smem = pl.BlockSpec(memory_space=pltpu.SMEM)
    sends = jnp.pad(send_list, (0, 768 - LANES * SLOTS)).reshape(1, 768)
    blocks = pl.pallas_call(
        functools.partial(exchange_kernel, nx, ny, nz),
        out_shape=jax.ShapeDtypeStruct((27, ROWS, POINTS), BF16),
        in_specs=[smem, vmem, vmem, vmem],
        out_specs=vmem,
        scratch_shapes=[
            pltpu.VMEM((16, 256), F32),
            pltpu.SemaphoreType.DMA((26,)),
            pltpu.SemaphoreType.DMA((27,)),
        ],
        compiler_params=pltpu.CompilerParams(
            collective_id=0, has_side_effects=True, vmem_limit_bytes=32 * 1024 * 1024
        ),
        name="exchange",
    )(pair_count, pairs, sends, multipoles)
    width_m = PAIRS + LANES * 64
    return pl.pallas_call(
        compute_kernel,
        out_shape=jax.ShapeDtypeStruct((BOXES, POINTS), F32),
        in_specs=[smem, vmem, vmem, vmem],
        out_specs=vmem,
        scratch_shapes=[
            pltpu.VMEM((27, 4, 8, 256), F32),
            pltpu.VMEM((27, 128), I32),
            pltpu.SMEM((27, 128), I32),
            pltpu.VMEM((8, LANES * 64), F32),
            pltpu.VMEM((768, POINTS), BF16),
            pltpu.VMEM((PAIRS, POINTS), BF16),
            pltpu.VMEM((width_m, POINTS), BF16),
            pltpu.VMEM((1, width_m), I32),
            pltpu.VMEM((1024, POINTS), F32),
            pltpu.SemaphoreType.DMA,
        ],
        compiler_params=pltpu.CompilerParams(vmem_limit_bytes=48 * 1024 * 1024),
        name="compute",
    )(pair_count, pairs, blocks, operators)


def solution(mesh):
    shape = dict(mesh.shape)
    ny = min(8, shape["gx"] // 2)
    sizes = (shape["gy"], ny, shape["gx"] // ny)
    return jax.shard_map(
        functools.partial(local, sizes),
        mesh=mesh,
        in_specs=(
            P(("gx", "gy"), None),
            P(),
            P(None, ("gx", "gy")),
            P(("gx", "gy")),
            P(("gx", "gy")),
        ),
        out_specs=P(("gx", "gy"), None),
        check_vma=False,
    )
```

```python
import functools

import jax
import jax.numpy as jnp
from jax import lax
from jax.experimental import pallas as pl
from jax.experimental.pallas import tpu as pltpu
from jax.sharding import PartitionSpec as P

MESH = pl.DeviceIdType.MESH
F32 = jnp.float32
BF16 = jnp.bfloat16
I32 = jnp.int32

BOXES = 64
POINTS = 256
PAIRS = 1024
LANES = 26
SLOTS = 24
OPS = 16
OWN = 13
ROWS = 80
WINDOW = 64


ORDER = list(range(9, 17)) + list(range(0, 9)) + list(range(17, 26))
GROUPS = [ORDER[0:4], ORDER[4:8], ORDER[8:12], ORDER[12:16], ORDER[16:20], ORDER[20:24], ORDER[24:26]]
EARLY = 2


def code_of(lane):
    return lane if lane < OWN else lane + 1


def heading(code):
    return code // 9 - 1, code // 3 % 3 - 1, code % 3 - 1


def iota(shape, axis):
    return lax.broadcasted_iota(I32, shape, axis)


def one_hot(condition):
    return jnp.where(condition, 1.0, 0.0).astype(BF16)


def nt(a, b):
    return lax.dot_general(a, b, (((1,), (1,)), ((), ())), preferred_element_type=F32)


def mm(a, b):
    return jnp.dot(a, b, preferred_element_type=F32)


def pack_pairs(count, pairs_ref, send_ref, tail, meta):
    source = pairs_ref[0:1, :]
    target = pairs_ref[1:2, :]
    operator = pairs_ref[2:3, :]
    used = iota((1, PAIRS), 1) < count
    ghost = jnp.maximum(source - BOXES, 0)
    lane = jnp.right_shift(ghost * 2731, 16)
    slot = ghost - lane * SLOTS
    lane = jnp.where(used, jnp.where(source < BOXES, LANES, lane), 31)
    codes = iota((32, PAIRS), 0)
    start = jnp.sum(jnp.where(lane < codes, 1.0, 0.0), axis=1, keepdims=True)
    before = one_hot(iota((128, 128), 0) < iota((128, 128), 1))
    carry = start
    places = []
    for chunk in range(PAIRS // 128):
        hot = jnp.where(codes[:, :128] == lane[:, chunk * 128:(chunk + 1) * 128], 1.0, 0.0)
        rank = mm(hot.astype(BF16), before) + carry
        places.append(jnp.sum(hot * rank, axis=0, keepdims=True))
        carry = carry + jnp.sum(hot, axis=1, keepdims=True)
    place = jnp.concatenate(places, axis=1).astype(I32)
    fields = jnp.concatenate(
        [slot, target, operator, jnp.zeros((5, PAIRS), I32)], axis=0
    ).astype(F32).astype(BF16)
    for q in range(4):
        hot = one_hot(iota((256, PAIRS), 0) + 256 * q == place)
        ordered = nt(fields, hot)
        meta[4 * q:4 * q + 3, :] = ordered[0:3, :]
    sends = send_ref[...].astype(F32)
    meta[3:4, :] = sends[:, 0:256]
    meta[7:8, :] = sends[:, 256:512]
    meta[11:12, 0:112] = sends[:, 512:624]
    meta[11:12, 112:256] = jnp.zeros((1, 144), F32)
    diagonal = iota((32, 128), 0) == iota((32, 128), 1)
    starts = jnp.sum(jnp.where(diagonal, start, 0.0), axis=0, keepdims=True).astype(I32)
    high = jnp.right_shift(starts, 5)
    meta[15:16, 0:128] = high.astype(F32)
    meta[15:16, 128:256] = (starts - high * 32).astype(F32)
    tail[...] = meta[...].astype(BF16)


def split(value):
    high = value.astype(BF16)
    return high, (value - high.astype(F32)).astype(BF16)


def count_own(count, pairs_ref, own_counts, hot_t):
    source = pairs_ref[0:1, :]
    target = pairs_ref[1:2, :]
    operator = pairs_ref[2:3, :]
    used = jnp.logical_and(iota((1, PAIRS), 1) < count, source < BOXES)
    key = jnp.where(used, operator * BOXES + source, -1)
    hot_t[...] = one_hot(iota((BOXES, PAIRS), 0) == target)
    for q in range(4):
        hot = one_hot(iota((256, PAIRS), 0) + 256 * q == key)
        high, low = split(nt(hot, hot_t[...]))
        own_counts[256 * q:256 * (q + 1), :] = jnp.concatenate([high, low], axis=1)


def count_forward(count, pairs_ref, counts, hot_u):
    source = pairs_ref[0:1, :]
    target = pairs_ref[1:2, :]
    operator = pairs_ref[2:3, :]
    used = iota((1, PAIRS), 1) < count
    key = jnp.where(used, operator * BOXES + target, -1)
    low, high = BOXES + 9 * SLOTS, BOXES + 17 * SLOTS
    moved = jnp.where(source < low, source + 8 * SLOTS, jnp.where(source < high, source - 9 * SLOTS, source))
    hot_u[...] = one_hot(iota((768, PAIRS), 0) == jnp.where(source < BOXES, source, moved))
    for q in range(4):
        hot = one_hot(iota((256, PAIRS), 0) + 256 * q == key)
        for c in range(3):
            high, low = split(nt(hot, hot_u[256 * c:256 * (c + 1), :]))
            counts[256 * q:256 * (q + 1), 256 * c:256 * (c + 1)] = high
            counts[256 * q:256 * (q + 1), 768 + 256 * c:768 + 256 * (c + 1)] = low


def column(row):
    n = row.shape[1]
    parts = []
    for c in range(n // 128):
        piece = jnp.broadcast_to(row[:, c * 128:(c + 1) * 128], (8, 128))
        parts.append(jnp.transpose(piece)[:, 0:1])
    return jnp.concatenate(parts, axis=0)


def unpack(blocks, code, meta, starts_v):
    wide = blocks[code, BOXES:ROWS, :].astype(F32)
    for q in range(4):
        meta[code, q, 0:4, :] = wide[4 * q:4 * q + 4, :]
        meta[code, q, 4:8, :] = wide[4 * q:4 * q + 4, :]
    starts_v[code:code + 1, :] = (wide[15:16, 0:128] * 32.0 + wide[15:16, 128:256]).astype(I32)


def longest_lane(starts):
    lengths = pltpu.roll(starts, 127, 1) - starts
    code = iota((32, 128), 0)
    back = LANES - 1 - jnp.where(code < OWN, code, code - 1)
    theirs = jnp.logical_and(iota((32, 128), 1) == back, jnp.logical_and(code != OWN, code < 27))
    lengths = jnp.where(theirs, lengths, 0).astype(F32)
    return jnp.max(jnp.max(lengths, axis=0, keepdims=True), axis=1, keepdims=True)


def window(meta, code, begin, offset):
    begin = jnp.minimum(begin, PAIRS - 1)
    chunk = lax.div(begin, 128)
    after = jnp.minimum(chunk + 1, 7)

    def piece(c):
        return meta[code, lax.div(c, 2), :, pl.ds(pl.multiple_of(lax.rem(c, 2) * 128, 128), 128)]

    shift = begin - chunk * 128
    turn = lax.rem(256 + offset - shift, 128)
    first = pltpu.roll(piece(chunk), turn, 1)
    second = pltpu.roll(piece(after), turn, 1)
    return jnp.where(iota((8, 128), 1) < 128 - shift + offset, first, second)


def gather_ghosts(blocks, group, meta, ghost):
    width = 64 * len(group)
    table = jnp.concatenate([blocks[code_of(lane), 0:BOXES, :] for lane in group], axis=0)
    picks = []
    for i, lane in enumerate(group):
        low = lane * SLOTS
        q, at = low // 128, low % 128
        cells = [meta[code_of(lane), p // 2, 3:4, p % 2 * 128:p % 2 * 128 + 128] for p in (q, min(q + 1, 5))]
        both = column(jnp.concatenate(cells, axis=1))
        picked = both[at:at + SLOTS, :].astype(I32) + 64 * i
        picks.append(jnp.where(iota((SLOTS, width), 1) == picked, 1.0, 0.0))
    hot = jnp.concatenate(picks, axis=0).astype(BF16)
    first = BOXES + SLOTS * ORDER.index(group[0])
    ghost[first:first + SLOTS * len(group), :] = mm(hot, table).astype(BF16)


def gather_events(blocks, group, meta, starts_v, own_boxes, events, keys_m, rows_m):
    base = 64 * ORDER.index(group[0])
    across = iota((8, 128), 1)
    upper = iota((8, 128), 0) < 4
    left = across < 64

    def pick(first, second):
        return jnp.where(upper, first, second)

    for pair in range(len(group) // 2):
        codes = [code_of(lane) for lane in group[2 * pair:2 * pair + 2]]
        backs = [LANES - 1 - lane for lane in group[2 * pair:2 * pair + 2]]
        start = [starts_v[c:c + 1, b:b + 1] for c, b in zip(codes, backs)]
        after = [starts_v[c:c + 1, b + 1:b + 2] for c, b in zip(codes, backs)]
        begin = jnp.minimum(pick(*start), PAIRS - 1)
        offset = pick(jnp.int32(0), jnp.int32(64))
        chunk = jnp.right_shift(begin, 7)
        shift = begin - chunk * 128
        chunks = [
            pick(*[meta[c, p // 2, :, p % 2 * 128:p % 2 * 128 + 128] for c in codes]) for p in range(8)
        ]
        now, later = chunks[0], chunks[1]
        for p in range(1, 8):
            here = chunk == p
            now = jnp.where(here, chunks[p], now)
            later = jnp.where(here, chunks[min(p + 1, 7)], later)
        amount = jnp.bitwise_and(shift - offset + 128, 127)
        for bit in range(7):
            turned = jnp.bitwise_and(amount, 1 << bit) != 0
            now = jnp.where(turned, pltpu.roll(now, 128 - (1 << bit), 1), now)
            later = jnp.where(turned, pltpu.roll(later, 128 - (1 << bit), 1), later)
        part = jnp.where(across < 128 - shift + offset, now, later)
        part = jnp.where(left, part, pltpu.roll(part, 4, 0))
        hot = iota((SLOTS, 128), 0) == part[0:1, :].astype(I32)
        theirs = [own_boxes[b * SLOTS:(b + 1) * SLOTS, :] for b in backs]
        theirs = jnp.where(iota((SLOTS, 128), 1) < 64, *theirs)
        box = jnp.sum(jnp.where(hot, theirs, 0.0), axis=0, keepdims=True)
        key = (part[2:3, :] * BOXES + box).astype(I32)
        flat = iota((1, 128), 1)
        length = jnp.where(flat < 64, after[0] - start[0], after[1] - start[1])
        span = slice(base + pair * 128, base + (pair + 1) * 128)
        events[:, span] = part
        keys_m[0:1, span] = jnp.where(jnp.where(flat < 64, flat, flat - 64) < length, key, -1)
    width = 64 * len(group)
    table = jnp.concatenate([blocks[code_of(lane), 0:BOXES, :] for lane in group], axis=0)
    targets = column(events[1:2, base:base + width]).astype(I32)
    which = jnp.right_shift(iota((width, 1), 0), 6)
    hot = one_hot(iota((width, width), 1) == targets + 64 * which)
    rows_m[base:base + width, :] = mm(hot, table).astype(BF16)


def apply_operators(total, forward, mirror, ops_ref, q):
    if forward is not None:
        f_high, f_low = split(forward)
    m_high, m_low = split(mirror)
    for i in range(4):
        part = slice(64 * i, 64 * i + 64)
        matrix = ops_ref[4 * q + i]
        if forward is not None:
            total += mm(jnp.concatenate([f_high[part], f_low[part]], axis=0), matrix)
        total += nt(jnp.concatenate([m_high[part], m_low[part]], axis=0), matrix)
    return total


def remainder_kernel(field_hbm, blocks_hbm, ops_hbm, out_hbm, field, blocks, ops_ref, meta, starts_v, starts_s, zm, sem):
    fetch = pltpu.make_async_copy(field_hbm.at[pl.ds(BOXES, 8)], field.at[pl.ds(BOXES, 8)], sem.at[0])
    through = pltpu.make_async_copy(field_hbm.at[pl.ds(0, BOXES)], out_hbm, sem.at[1])
    fetch.start()
    through.start()
    fetch.wait()
    through.wait()

    @pl.when(jnp.max(field[BOXES:, :]) > WINDOW)
    def _():
        loads = [
            pltpu.make_async_copy(field_hbm, field, sem.at[0]),
            pltpu.make_async_copy(blocks_hbm, blocks, sem.at[1]),
            pltpu.make_async_copy(ops_hbm, ops_ref, sem.at[2]),
        ]
        for load in loads:
            load.start()
        for load in loads:
            load.wait()
        for code in range(27):
            unpack(blocks, code, meta, starts_v)
        copy = pltpu.make_async_copy(starts_v, starts_s, sem.at[3])
        copy.start()
        copy.wait()
        own_boxes = column(jnp.concatenate([meta[OWN, q, 3:4, :] for q in range(3)], axis=1))
        zm[...] = jnp.zeros_like(zm)

        @pl.loop(0, LANES)
        def _(lane):
            code = jnp.where(lane < OWN, lane, lane + 1)
            back = LANES - 1 - lane
            begin = starts_s[code, back]
            length = starts_s[code, back + 1] - begin

            @pl.loop(1, lax.div(length + WINDOW - 1, WINDOW))
            def _(turn):
                part = window(meta, code, begin + turn * WINDOW, 0)
                boxes_row = jnp.zeros((1, 128), F32)
                slots = part[0:1, :].astype(I32) + back * SLOTS
                for q in range(6):
                    hot = iota((128, 128), 0) + 128 * q == slots
                    spread = own_boxes[q * 128:(q + 1) * 128, :]
                    boxes_row += jnp.sum(jnp.where(hot, spread, 0.0), axis=0, keepdims=True)
                key = (part[2:3, :] * BOXES + boxes_row).astype(I32)
                key = jnp.where(iota((1, 128), 1) < jnp.minimum(length - turn * WINDOW, WINDOW), key, -1)
                hot = one_hot(iota((128, BOXES), 1) == column(part[1:2, :]).astype(I32))
                rows = mm(hot, blocks[code, 0:BOXES, :]).astype(BF16)
                for q in range(4):
                    hot = one_hot(iota((256, 128), 0) + 256 * q == key)
                    zm[256 * q:256 * (q + 1), :] += mm(hot, rows)

        total = jnp.zeros((128, POINTS), F32)
        for q in range(4):
            total = apply_operators(total, None, zm[256 * q:256 * (q + 1), :], ops_ref, q)
        field[0:BOXES, :] += total[0:BOXES, :] + total[BOXES:, :]
        store = pltpu.make_async_copy(field.at[pl.ds(0, BOXES)], out_hbm, sem.at[1])
        store.start()
        store.wait()


def main_kernel(
    nx, ny, nz, count_ref, pairs_hbm, send_hbm, m_hbm, ops_hbm,
    field_ref, blocks_hbm,
    blocks, ops_ref, counts, own_counts, pairs_ref, send_ref, tail, hot_t, hot_u,
    meta, starts_v, events, keys_m, ghost, rows_m, zf, zm,
    in_sem, send_sem, recv_sem,
):
    g = lax.axis_index("gx")
    h = lax.axis_index("gy")
    by = lax.rem(g, ny)
    bz = lax.div(g, ny)
    steps = {
        "z": {1: bz < nz - 1, -1: bz > 0, 0: True},
        "y": {1: by < ny - 1, -1: by > 0, 0: True},
        "x": {1: h < nx - 1, -1: h > 0, 0: True},
    }
    partner = {
        "z": lambda s: (g + s * ny, h),
        "y": lambda s: (g + s, h),
        "x": lambda s: (g, h + s),
    }

    def on_grid(dx, dy, dz):
        cond = None
        for flag in (steps["x"][dx], steps["y"][dy], steps["z"][dz]):
            if flag is not True:
                cond = flag if cond is None else jnp.logical_and(cond, flag)
        return cond

    barrier = pltpu.get_barrier_semaphore()
    for axis in "zyx":
        for s in (1, -1):
            @pl.when(steps[axis][s])
            def _():
                pl.semaphore_signal(barrier, inc=1, device_id=partner[axis](s), device_id_type=MESH)

    loads = [
        pltpu.make_async_copy(src, dst, in_sem.at[i])
        for i, (src, dst) in enumerate([
            (pairs_hbm, pairs_ref),
            (send_hbm, send_ref),
            (m_hbm, blocks.at[OWN, pl.ds(0, BOXES)]),
            (ops_hbm, ops_ref),
        ])
    ]
    for load in loads:
        load.start()

    pl.semaphore_wait(
        barrier,
        sum(steps[axis][s].astype(I32) for axis in "zyx" for s in (1, -1)),
    )

    def as_code(dx, dy, dz):
        return (dx + 1) * 9 + (dy + 1) * 3 + dz + 1

    spans = [pl.ds(0, BOXES), pl.ds(BOXES, ROWS - BOXES)]
    started = []

    def send(src, axis, s, part):
        dx, dy, dz = src
        dst = {"x": (-s, dy, dz), "y": (dx, -s, dz), "z": (dx, dy, -s)}[axis]
        need = {"x": (s, dy, dz), "y": (dx, s, dz), "z": (dx, dy, s)}[axis]
        cond = on_grid(*need)
        own = src == (0, 0, 0) and part == 0
        copy = pltpu.make_async_remote_copy(
            src_ref=m_hbm if own else blocks.at[as_code(*src), spans[part]],
            dst_ref=blocks.at[as_code(*dst), spans[part]],
            send_sem=send_sem.at[len(started)],
            recv_sem=recv_sem.at[part, as_code(*dst)],
            device_id=partner[axis](s),
            device_id_type=MESH,
        )
        started.append((copy, cond))
        pl.when(cond)(copy.start)

    def arrived(where, part):
        code = as_code(*where)
        slot = blocks.at[code, spans[part]]
        copy = pltpu.make_async_remote_copy(
            src_ref=slot, dst_ref=slot, send_sem=send_sem.at[0], recv_sem=recv_sem.at[part, code],
            device_id=(g, h), device_id_type=MESH,
        )
        pl.when(on_grid(*where))(copy.wait_recv)

    def send_home(part):
        for axis in "zyx":
            for s in (1, -1):
                send((0, 0, 0), axis, s, part)

    def relay(places, axes, part):
        for where in places:
            arrived(where, part)
            for axis in axes:
                for s in (1, -1):
                    send(where, axis, s, part)

    along_y = [(0, 1, 0), (0, -1, 0)]
    along_z = [(0, 0, 1), (0, 0, -1)]
    along_yz = [(0, 1, 1), (0, -1, 1), (0, 1, -1), (0, -1, -1)]
    count = count_ref[0]
    send_home(0)
    loads[0].wait()
    loads[1].wait()
    pack_pairs(count, pairs_ref, send_ref, blocks.at[OWN, spans[1]], tail)
    send_home(1)
    for code in range(27):
        if code != OWN:
            @pl.when(jnp.logical_not(on_grid(*heading(code))))
            def _():
                blocks[code] = jnp.zeros((ROWS, POINTS), BF16)
    starts_v[27:32, :] = jnp.zeros((5, 128), I32)
    ghost[BOXES + LANES * SLOTS:, :] = jnp.zeros((768 - BOXES - LANES * SLOTS, POINTS), BF16)
    own_boxes = column(
        jnp.concatenate([tail[4 * q + 3:4 * q + 4, :] for q in range(3)], axis=1)
    )
    count_own(count, pairs_ref, own_counts, hot_t)
    count_forward(count, pairs_ref, counts, hot_u)
    relay(along_y, "x", 0)
    relay(along_z, "yx", 0)
    relay(along_y, "x", 1)
    relay(along_z, "yx", 1)
    relay(along_yz, "x", 0)
    relay(along_yz, "x", 1)
    loads[2].wait()
    loads[3].wait()

    def take(groups):
        for lane in sum(groups, []):
            unpack(blocks, code_of(lane), meta, starts_v)
        for group in groups:
            gather_ghosts(blocks, group, meta, ghost)
        for group in groups:
            gather_events(blocks, group, meta, starts_v, own_boxes, events, keys_m, rows_m)

    ghost[0:BOXES, :] = blocks[OWN, 0:BOXES, :]
    starts_v[0:27, :] = jnp.zeros((27, 128), I32)
    take(GROUPS[:EARLY])
    own = blocks[OWN, 0:BOXES, :]
    own_twice = jnp.concatenate([own, own], axis=0)
    cut = EARLY * 256
    quarters = [slice(256 * q, 256 * (q + 1)) for q in range(4)]
    for q, span in enumerate(quarters):
        zf[span, :] = mm(counts[span, 0:256], ghost[0:256, :]) + mm(counts[span, 768:1024], ghost[0:256, :])
        hot = one_hot(iota((256, cut), 0) + 256 * q == keys_m[:, 0:cut])
        zm[span, :] = mm(hot, rows_m[0:cut, :]) + mm(own_counts[span, :], own_twice)

    for part in range(2):
        for code in range(27):
            if heading(code)[0] != 0:
                arrived(heading(code), part)
    save = pltpu.make_async_copy(blocks, blocks_hbm, in_sem.at[4])
    save.start()
    take(GROUPS[EARLY:])
    total = jnp.zeros((128, POINTS), F32)
    for q, span in enumerate(quarters):
        forward = zf[span, :] + mm(counts[span, 256:768], ghost[256:768, :])
        forward += mm(counts[span, 1024:1536], ghost[256:768, :])
        hot = one_hot(iota((256, LANES * 64 - cut), 0) + 256 * q == keys_m[:, cut:])
        mirror = zm[span, :] + mm(hot, rows_m[cut:, :])
        total = apply_operators(total, forward, mirror, ops_ref, q)
    field_ref[0:BOXES, :] = total[0:BOXES, :] + total[BOXES:, :]
    field_ref[BOXES:, :] = jnp.full((8, POINTS), 0.0, F32) + longest_lane(starts_v[...])
    save.wait()
    for copy, cond in started:
        pl.when(cond)(copy.wait_send)


def local(sizes, multipoles, operators, pairs, pair_count, send_list):
    nx, ny, nz = sizes
    smem = pl.BlockSpec(memory_space=pltpu.SMEM)
    vmem = pl.BlockSpec(memory_space=pltpu.VMEM)
    anywhere = pl.BlockSpec(memory_space=pl.ANY)
    blocks_shape = (27, ROWS, POINTS)
    field, blocks = pl.pallas_call(
        functools.partial(main_kernel, nx, ny, nz),
        out_shape=[
            jax.ShapeDtypeStruct((BOXES + 8, POINTS), F32),
            jax.ShapeDtypeStruct(blocks_shape, BF16),
        ],
        in_specs=[smem, anywhere, anywhere, anywhere, anywhere],
        out_specs=[vmem, anywhere],
        scratch_shapes=[
            pltpu.VMEM(blocks_shape, BF16),
            pltpu.VMEM((OPS, POINTS, POINTS), BF16),
            pltpu.VMEM((1024, 1536), BF16),
            pltpu.VMEM((1024, 128), BF16),
            pltpu.VMEM((3, PAIRS), I32),
            pltpu.VMEM((1, LANES * SLOTS), I32),
            pltpu.VMEM((16, 256), F32),
            pltpu.VMEM((BOXES, PAIRS), BF16),
            pltpu.VMEM((768, PAIRS), BF16),
            pltpu.VMEM((27, 4, 8, 256), F32),
            pltpu.VMEM((32, 128), I32),
            pltpu.VMEM((8, LANES * 64), F32),
            pltpu.VMEM((1, LANES * 64), I32),
            pltpu.VMEM((768, POINTS), BF16),
            pltpu.VMEM((LANES * 64, POINTS), BF16),
            pltpu.VMEM((1024, POINTS), F32),
            pltpu.VMEM((1024, POINTS), F32),
            pltpu.SemaphoreType.DMA((5,)),
            pltpu.SemaphoreType.DMA((52,)),
            pltpu.SemaphoreType.DMA((2, 27)),
        ],
        compiler_params=pltpu.CompilerParams(
            collective_id=0, has_side_effects=True, vmem_limit_bytes=58 * 1024 * 1024
        ),
        name="exchange",
    )(pair_count, pairs, send_list.reshape(1, LANES * SLOTS), multipoles, operators)
    return pl.pallas_call(
        remainder_kernel,
        out_shape=jax.ShapeDtypeStruct((BOXES, POINTS), F32),
        in_specs=[anywhere] * 3,
        out_specs=anywhere,
        scratch_shapes=[
            pltpu.VMEM((BOXES + 8, POINTS), F32),
            pltpu.VMEM(blocks_shape, BF16),
            pltpu.VMEM((OPS, POINTS, POINTS), BF16),
            pltpu.VMEM((27, 4, 8, 256), F32),
            pltpu.VMEM((32, 128), I32),
            pltpu.SMEM((32, 128), I32),
            pltpu.VMEM((1024, POINTS), F32),
            pltpu.SemaphoreType.DMA((4,)),
        ],
        compiler_params=pltpu.CompilerParams(vmem_limit_bytes=58 * 1024 * 1024),
        name="remainder",
    )(field, blocks, operators)


def solution(mesh):
    shape = dict(mesh.shape)
    ny = min(8, shape["gx"] // 2)
    sizes = (shape["gy"], ny, shape["gx"] // ny)
    return jax.shard_map(
        functools.partial(local, sizes),
        mesh=mesh,
        in_specs=(
            P(("gx", "gy"), None),
            P(),
            P(None, ("gx", "gy")),
            P(("gx", "gy")),
            P(("gx", "gy")),
        ),
        out_specs=P(("gx", "gy"), None),
        check_vma=False,
    )
```

```python
import functools

import jax
import jax.numpy as jnp
from jax import lax
from jax.experimental import pallas as pl
from jax.experimental.pallas import tpu as pltpu
from jax.sharding import PartitionSpec as P

MESH = pl.DeviceIdType.MESH
F32 = jnp.float32
BF16 = jnp.bfloat16
I32 = jnp.int32

BOXES = 64
POINTS = 256
PAIRS = 1024
LANES = 26
SLOTS = 24
OPS = 16
OWN = 13
ROWS = 80
WINDOW = 64


EARLY = [9, 10, 11, 12, 13, 14, 15, 16]
MIDDLE = [4, 21, 1, 3, 5, 7, 18, 20, 22, 24]
CORNERS = [0, 2, 6, 8, 17, 19, 23, 25]
ORDER = EARLY + MIDDLE + CORNERS
MID, LATE = 64 * len(EARLY), 64 * len(EARLY + MIDDLE)


def quads(lanes):
    return [lanes[i:i + 4] for i in range(0, len(lanes), 4)]


def ghost_row(lane):
    return BOXES + SLOTS * ORDER.index(lane) + (16 if lane in CORNERS else 0)


def code_of(lane):
    return lane if lane < OWN else lane + 1


def heading(code):
    return code // 9 - 1, code // 3 % 3 - 1, code % 3 - 1


def iota(shape, axis):
    return lax.broadcasted_iota(I32, shape, axis)


def one_hot(condition):
    return jnp.where(condition, 1.0, 0.0).astype(BF16)


def nt(a, b):
    return lax.dot_general(a, b, (((1,), (1,)), ((), ())), preferred_element_type=F32)


def mm(a, b):
    return jnp.dot(a, b, preferred_element_type=F32)


def pack_pairs(count, pairs_ref, send_ref, tail, meta):
    source = pairs_ref[0:1, :]
    target = pairs_ref[1:2, :]
    operator = pairs_ref[2:3, :]
    used = iota((1, PAIRS), 1) < count
    ghost = jnp.maximum(source - BOXES, 0)
    lane = jnp.right_shift(ghost * 2731, 16)
    slot = ghost - lane * SLOTS
    lane = jnp.where(used, jnp.where(source < BOXES, LANES, lane), 31)
    codes = iota((32, PAIRS), 0)
    start = jnp.sum(jnp.where(lane < codes, 1.0, 0.0), axis=1, keepdims=True)
    before = one_hot(iota((128, 128), 0) < iota((128, 128), 1))
    carry = start
    places = []
    for chunk in range(PAIRS // 128):
        hot = jnp.where(codes[:, :128] == lane[:, chunk * 128:(chunk + 1) * 128], 1.0, 0.0)
        rank = mm(hot.astype(BF16), before) + carry
        places.append(jnp.sum(hot * rank, axis=0, keepdims=True))
        carry = carry + jnp.sum(hot, axis=1, keepdims=True)
    place = jnp.concatenate(places, axis=1).astype(I32)
    fields = jnp.concatenate(
        [slot, target, operator, jnp.zeros((5, PAIRS), I32)], axis=0
    ).astype(F32).astype(BF16)
    for q in range(4):
        hot = one_hot(iota((256, PAIRS), 0) + 256 * q == place)
        ordered = nt(fields, hot)
        meta[4 * q:4 * q + 3, :] = ordered[0:3, :]
    sends = send_ref[...].reshape(1, LANES * SLOTS).astype(F32)
    meta[3:4, :] = sends[:, 0:256]
    meta[7:8, :] = sends[:, 256:512]
    meta[11:12, 0:112] = sends[:, 512:624]
    meta[11:12, 112:256] = jnp.zeros((1, 144), F32)
    diagonal = iota((32, 128), 0) == iota((32, 128), 1)
    starts = jnp.sum(jnp.where(diagonal, start, 0.0), axis=0, keepdims=True).astype(I32)
    high = jnp.right_shift(starts, 5)
    meta[15:16, 0:128] = high.astype(F32)
    meta[15:16, 128:256] = (starts - high * 32).astype(F32)
    tail[...] = meta[...].astype(BF16)


def split(value):
    high = value.astype(BF16)
    return high, (value - high.astype(F32)).astype(BF16)


def count_own(count, pairs_ref, own_counts, hot_t):
    source = pairs_ref[0:1, :]
    target = pairs_ref[1:2, :]
    operator = pairs_ref[2:3, :]
    used = jnp.logical_and(iota((1, PAIRS), 1) < count, source < BOXES)
    key = jnp.where(used, operator * BOXES + source, -1)
    hot_t[...] = one_hot(iota((BOXES, PAIRS), 0) == target)
    for q in range(4):
        hot = one_hot(iota((256, PAIRS), 0) + 256 * q == key)
        high, low = split(nt(hot, hot_t[...]))
        own_counts[256 * q:256 * (q + 1), :] = jnp.concatenate([high, low], axis=1)


def count_forward(count, pairs_ref, counts, hot_u):
    source = pairs_ref[0:1, :]
    target = pairs_ref[1:2, :]
    operator = pairs_ref[2:3, :]
    used = iota((1, PAIRS), 1) < count
    key = jnp.where(used, operator * BOXES + target, -1)
    move = jnp.zeros((1, PAIRS), I32)
    for lane in range(LANES):
        first = BOXES + SLOTS * lane
        move = jnp.where(source >= first, ghost_row(lane) - first, move)
    hot_u[...] = one_hot(iota((768, PAIRS), 0) == source + move)
    for q in range(4):
        hot = one_hot(iota((256, PAIRS), 0) + 256 * q == key)
        for c in range(3):
            high, low = split(nt(hot, hot_u[256 * c:256 * (c + 1), :]))
            counts[256 * q:256 * (q + 1), 256 * c:256 * (c + 1)] = high
            counts[256 * q:256 * (q + 1), 768 + 256 * c:768 + 256 * (c + 1)] = low


def column(row):
    n = row.shape[1]
    parts = []
    for c in range(n // 128):
        piece = jnp.broadcast_to(row[:, c * 128:(c + 1) * 128], (8, 128))
        parts.append(jnp.transpose(piece)[:, 0:1])
    return jnp.concatenate(parts, axis=0)


def unpack(blocks, code, meta, starts_v):
    wide = blocks[code, BOXES:ROWS, :].astype(F32)
    for q in range(4):
        meta[code, q, 0:4, :] = wide[4 * q:4 * q + 4, :]
        meta[code, q, 4:8, :] = wide[4 * q:4 * q + 4, :]
    starts_v[code:code + 1, :] = (wide[15:16, 0:128] * 32.0 + wide[15:16, 128:256]).astype(I32)


def longest_lane(starts):
    lengths = pltpu.roll(starts, 127, 1) - starts
    code = iota((32, 128), 0)
    back = LANES - 1 - jnp.where(code < OWN, code, code - 1)
    theirs = jnp.logical_and(iota((32, 128), 1) == back, jnp.logical_and(code != OWN, code < 27))
    lengths = jnp.where(theirs, lengths, 0).astype(F32)
    return jnp.max(jnp.max(lengths, axis=0, keepdims=True), axis=1, keepdims=True)


def window(meta, code, begin, offset):
    begin = jnp.minimum(begin, PAIRS - 1)
    chunk = lax.div(begin, 128)
    after = jnp.minimum(chunk + 1, 7)

    def piece(c):
        return meta[code, lax.div(c, 2), :, pl.ds(pl.multiple_of(lax.rem(c, 2) * 128, 128), 128)]

    shift = begin - chunk * 128
    turn = lax.rem(256 + offset - shift, 128)
    first = pltpu.roll(piece(chunk), turn, 1)
    second = pltpu.roll(piece(after), turn, 1)
    return jnp.where(iota((8, 128), 1) < 128 - shift + offset, first, second)


def gather_ghosts(blocks, group, meta, ghost):
    width = 64 * len(group)
    table = jnp.concatenate([blocks[code_of(lane), 0:BOXES, :] for lane in group], axis=0)
    picks = []
    for i, lane in enumerate(group):
        low = lane * SLOTS
        q, at = low // 128, low % 128
        cells = [meta[code_of(lane), p // 2, 3:4, p % 2 * 128:p % 2 * 128 + 128] for p in (q, min(q + 1, 5))]
        both = column(jnp.concatenate(cells, axis=1))
        picked = both[at:at + SLOTS, :].astype(I32) + 64 * i
        picks.append(jnp.where(iota((SLOTS, width), 1) == picked, 1.0, 0.0))
    hot = jnp.concatenate(picks, axis=0).astype(BF16)
    first = ghost_row(group[0])
    ghost[first:first + SLOTS * len(group), :] = mm(hot, table).astype(BF16)


def gather_events(blocks, group, meta, starts_v, own_boxes, events, keys_m, rows_m):
    base = 64 * ORDER.index(group[0])
    across = iota((8, 128), 1)
    upper = iota((8, 128), 0) < 4
    left = across < 64

    def pick(first, second):
        return jnp.where(upper, first, second)

    for pair in range(len(group) // 2):
        codes = [code_of(lane) for lane in group[2 * pair:2 * pair + 2]]
        backs = [LANES - 1 - lane for lane in group[2 * pair:2 * pair + 2]]
        start = [starts_v[c:c + 1, b:b + 1] for c, b in zip(codes, backs)]
        after = [starts_v[c:c + 1, b + 1:b + 2] for c, b in zip(codes, backs)]
        begin = jnp.minimum(pick(*start), PAIRS - 1)
        offset = pick(jnp.int32(0), jnp.int32(64))
        chunk = jnp.right_shift(begin, 7)
        shift = begin - chunk * 128
        chunks = [
            pick(*[meta[c, p // 2, :, p % 2 * 128:p % 2 * 128 + 128] for c in codes]) for p in range(8)
        ]
        now, later = chunks[0], chunks[1]
        for p in range(1, 8):
            here = chunk == p
            now = jnp.where(here, chunks[p], now)
            later = jnp.where(here, chunks[min(p + 1, 7)], later)
        amount = jnp.bitwise_and(shift - offset + 128, 127)
        for bit in range(7):
            turned = jnp.bitwise_and(amount, 1 << bit) != 0
            now = jnp.where(turned, pltpu.roll(now, 128 - (1 << bit), 1), now)
            later = jnp.where(turned, pltpu.roll(later, 128 - (1 << bit), 1), later)
        part = jnp.where(across < 128 - shift + offset, now, later)
        part = jnp.where(left, part, pltpu.roll(part, 4, 0))
        hot = iota((SLOTS, 128), 0) == part[0:1, :].astype(I32)
        theirs = [own_boxes[b * SLOTS:(b + 1) * SLOTS, :] for b in backs]
        theirs = jnp.where(iota((SLOTS, 128), 1) < 64, *theirs)
        box = jnp.sum(jnp.where(hot, theirs, 0.0), axis=0, keepdims=True)
        key = (part[2:3, :] * BOXES + box).astype(I32)
        flat = iota((1, 128), 1)
        length = jnp.where(flat < 64, after[0] - start[0], after[1] - start[1])
        span = slice(base + pair * 128, base + (pair + 1) * 128)
        events[:, span] = part
        keys_m[0:1, span] = jnp.where(jnp.where(flat < 64, flat, flat - 64) < length, key, -1)
    width = 64 * len(group)
    table = jnp.concatenate([blocks[code_of(lane), 0:BOXES, :] for lane in group], axis=0)
    targets = column(events[1:2, base:base + width]).astype(I32)
    which = jnp.right_shift(iota((width, 1), 0), 6)
    hot = one_hot(iota((width, width), 1) == targets + 64 * which)
    rows_m[base:base + width, :] = mm(hot, table).astype(BF16)


def apply_operators(total, forward, mirror, ops_ref, q):
    if forward is not None:
        f_high, f_low = split(forward)
    m_high, m_low = split(mirror)
    for i in range(4):
        part = slice(64 * i, 64 * i + 64)
        matrix = ops_ref[4 * q + i]
        if forward is not None:
            total += mm(jnp.concatenate([f_high[part], f_low[part]], axis=0), matrix)
        total += nt(jnp.concatenate([m_high[part], m_low[part]], axis=0), matrix)
    return total


def remainder_kernel(field_hbm, blocks_hbm, ops_hbm, out_hbm, field, blocks, ops_ref, meta, starts_v, starts_s, zm, sem):
    fetch = pltpu.make_async_copy(field_hbm, field, sem.at[0])
    fetch.start()
    fetch.wait()

    @pl.when(jnp.max(field[BOXES:, :]) > WINDOW)
    def _():
        loads = [
            pltpu.make_async_copy(blocks_hbm, blocks, sem.at[1]),
            pltpu.make_async_copy(ops_hbm, ops_ref, sem.at[2]),
        ]
        for load in loads:
            load.start()
        for load in loads:
            load.wait()
        for code in range(27):
            unpack(blocks, code, meta, starts_v)
        copy = pltpu.make_async_copy(starts_v, starts_s, sem.at[3])
        copy.start()
        copy.wait()
        own_boxes = column(jnp.concatenate([meta[OWN, q, 3:4, :] for q in range(3)], axis=1))
        zm[...] = jnp.zeros_like(zm)

        @pl.loop(0, LANES)
        def _(lane):
            code = jnp.where(lane < OWN, lane, lane + 1)
            back = LANES - 1 - lane
            begin = starts_s[code, back]
            length = starts_s[code, back + 1] - begin

            @pl.loop(1, lax.div(length + WINDOW - 1, WINDOW))
            def _(turn):
                part = window(meta, code, begin + turn * WINDOW, 0)
                boxes_row = jnp.zeros((1, 128), F32)
                slots = part[0:1, :].astype(I32) + back * SLOTS
                for q in range(6):
                    hot = iota((128, 128), 0) + 128 * q == slots
                    spread = own_boxes[q * 128:(q + 1) * 128, :]
                    boxes_row += jnp.sum(jnp.where(hot, spread, 0.0), axis=0, keepdims=True)
                key = (part[2:3, :] * BOXES + boxes_row).astype(I32)
                key = jnp.where(iota((1, 128), 1) < jnp.minimum(length - turn * WINDOW, WINDOW), key, -1)
                hot = one_hot(iota((128, BOXES), 1) == column(part[1:2, :]).astype(I32))
                rows = mm(hot, blocks[code, 0:BOXES, :]).astype(BF16)
                for q in range(4):
                    hot = one_hot(iota((256, 128), 0) + 256 * q == key)
                    zm[256 * q:256 * (q + 1), :] += mm(hot, rows)

        total = jnp.zeros((128, POINTS), F32)
        for q in range(4):
            total = apply_operators(total, None, zm[256 * q:256 * (q + 1), :], ops_ref, q)
        field[0:BOXES, :] += total[0:BOXES, :] + total[BOXES:, :]

    store = pltpu.make_async_copy(field.at[pl.ds(0, BOXES)], out_hbm, sem.at[0])
    store.start()
    store.wait()


def main_kernel(
    nx, ny, nz, count_ref, pairs_hbm, send_hbm, m_hbm, ops_hbm,
    field_ref, blocks_hbm,
    blocks, ops_ref, counts, own_counts, pairs_ref, send_ref, tail, hot_t, hot_u,
    meta, starts_v, events, keys_m, ghost, rows_m, zf, zm,
    in_sem, send_sem, recv_sem,
):
    g = lax.axis_index("gx")
    h = lax.axis_index("gy")
    by = lax.rem(g, ny)
    bz = lax.div(g, ny)
    steps = {
        "z": {1: bz < nz - 1, -1: bz > 0, 0: True},
        "y": {1: by < ny - 1, -1: by > 0, 0: True},
        "x": {1: h < nx - 1, -1: h > 0, 0: True},
    }
    partner = {
        "z": lambda s: (g + s * ny, h),
        "y": lambda s: (g + s, h),
        "x": lambda s: (g, h + s),
    }

    def on_grid(dx, dy, dz):
        cond = None
        for flag in (steps["x"][dx], steps["y"][dy], steps["z"][dz]):
            if flag is not True:
                cond = flag if cond is None else jnp.logical_and(cond, flag)
        return cond

    barrier = pltpu.get_barrier_semaphore()
    for axis in "zyx":
        for s in (1, -1):
            @pl.when(steps[axis][s])
            def _():
                pl.semaphore_signal(barrier, inc=1, device_id=partner[axis](s), device_id_type=MESH)

    loads = [
        pltpu.make_async_copy(src, dst, in_sem.at[i])
        for i, (src, dst) in enumerate([
            (pairs_hbm, pairs_ref),
            (send_hbm, send_ref),
            (m_hbm, blocks.at[OWN, pl.ds(0, BOXES)]),
            (ops_hbm, ops_ref),
        ])
    ]
    for load in loads:
        load.start()

    pl.semaphore_wait(
        barrier,
        sum(steps[axis][s].astype(I32) for axis in "zyx" for s in (1, -1)),
    )

    def as_code(dx, dy, dz):
        return (dx + 1) * 9 + (dy + 1) * 3 + dz + 1

    spans = [pl.ds(0, BOXES), pl.ds(BOXES, ROWS - BOXES)]
    started = []

    def send(src, axis, s, part):
        dx, dy, dz = src
        dst = {"x": (-s, dy, dz), "y": (dx, -s, dz), "z": (dx, dy, -s)}[axis]
        need = {"x": (s, dy, dz), "y": (dx, s, dz), "z": (dx, dy, s)}[axis]
        cond = on_grid(*need)
        own = src == (0, 0, 0) and part == 0
        copy = pltpu.make_async_remote_copy(
            src_ref=m_hbm if own else blocks.at[as_code(*src), spans[part]],
            dst_ref=blocks.at[as_code(*dst), spans[part]],
            send_sem=send_sem.at[len(started)],
            recv_sem=recv_sem.at[part, as_code(*dst)],
            device_id=partner[axis](s),
            device_id_type=MESH,
        )
        started.append((copy, cond))
        pl.when(cond)(copy.start)

    def arrived(where, part):
        code = as_code(*where)
        slot = blocks.at[code, spans[part]]
        copy = pltpu.make_async_remote_copy(
            src_ref=slot, dst_ref=slot, send_sem=send_sem.at[0], recv_sem=recv_sem.at[part, code],
            device_id=(g, h), device_id_type=MESH,
        )
        pl.when(on_grid(*where))(copy.wait_recv)

    def send_home(part):
        for axis in "zyx":
            for s in (1, -1):
                send((0, 0, 0), axis, s, part)

    def relay(places, axes, part):
        for where in places:
            arrived(where, part)
            for axis in axes:
                for s in (1, -1):
                    send(where, axis, s, part)

    along_y = [(0, 1, 0), (0, -1, 0)]
    along_z = [(0, 0, 1), (0, 0, -1)]
    along_yz = [(0, 1, 1), (0, -1, 1), (0, 1, -1), (0, -1, -1)]
    count = count_ref[0]
    send_home(0)
    loads[0].wait()
    loads[1].wait()
    pack_pairs(count, pairs_ref, send_ref, blocks.at[OWN, spans[1]], tail)
    send_home(1)
    for code in range(27):
        if code != OWN:
            @pl.when(jnp.logical_not(on_grid(*heading(code))))
            def _():
                blocks[code] = jnp.zeros((ROWS, POINTS), BF16)
    starts_v[27:32, :] = jnp.zeros((5, 128), I32)
    ghost[496:512, :] = jnp.zeros((16, POINTS), BF16)
    ghost[704:768, :] = jnp.zeros((64, POINTS), BF16)
    own_boxes = column(
        jnp.concatenate([tail[4 * q + 3:4 * q + 4, :] for q in range(3)], axis=1)
    )
    count_own(count, pairs_ref, own_counts, hot_t)
    count_forward(count, pairs_ref, counts, hot_u)
    relay(along_y, "x", 0)
    relay(along_z, "yx", 0)
    relay(along_y, "x", 1)
    relay(along_z, "yx", 1)
    relay(along_yz, "x", 0)
    relay(along_yz, "x", 1)
    loads[2].wait()
    loads[3].wait()

    def take(lanes):
        for lane in lanes:
            unpack(blocks, code_of(lane), meta, starts_v)
        for group in quads(lanes):
            gather_ghosts(blocks, group, meta, ghost)
        for group in quads(lanes):
            gather_events(blocks, group, meta, starts_v, own_boxes, events, keys_m, rows_m)

    def wait_for(lanes):
        for part in range(2):
            for lane in lanes:
                arrived(heading(code_of(lane)), part)

    def sums(q, low, high, first, last):
        span = slice(256 * q, 256 * (q + 1))
        forward = mm(counts[span, low:high], ghost[low:high, :])
        forward += mm(counts[span, 768 + low:768 + high], ghost[low:high, :])
        hot = one_hot(iota((256, last - first), 0) + 256 * q == keys_m[:, first:last])
        return forward, mm(hot, rows_m[first:last, :])

    ghost[0:BOXES, :] = blocks[OWN, 0:BOXES, :]
    starts_v[0:27, :] = jnp.zeros((27, 128), I32)
    take(EARLY)
    own = blocks[OWN, 0:BOXES, :]
    own_twice = jnp.concatenate([own, own], axis=0)
    quarters = [slice(256 * q, 256 * (q + 1)) for q in range(4)]
    for q, span in enumerate(quarters):
        forward, mirror = sums(q, 0, 256, 0, MID)
        zf[span, :] = forward
        zm[span, :] = mirror + mm(own_counts[span, :], own_twice)

    wait_for(MIDDLE)
    take(MIDDLE)
    for q, span in enumerate(quarters):
        forward, mirror = sums(q, 256, 512, MID, LATE)
        zf[span, :] += forward
        zm[span, :] += mirror

    wait_for(CORNERS)
    save = pltpu.make_async_copy(blocks, blocks_hbm, in_sem.at[4])
    save.start()
    take(CORNERS)
    total = jnp.zeros((128, POINTS), F32)
    for q, span in enumerate(quarters):
        forward, mirror = sums(q, 512, 768, LATE, 64 * LANES)
        total = apply_operators(total, zf[span, :] + forward, zm[span, :] + mirror, ops_ref, q)
    field_ref[0:BOXES, :] = total[0:BOXES, :] + total[BOXES:, :]
    field_ref[BOXES:, :] = jnp.full((8, POINTS), 0.0, F32) + longest_lane(starts_v[...])
    save.wait()
    for copy, cond in started:
        pl.when(cond)(copy.wait_send)


def local(sizes, multipoles, operators, pairs, pair_count, send_list):
    nx, ny, nz = sizes
    smem = pl.BlockSpec(memory_space=pltpu.SMEM)
    vmem = pl.BlockSpec(memory_space=pltpu.VMEM)
    anywhere = pl.BlockSpec(memory_space=pl.ANY)
    blocks_shape = (27, ROWS, POINTS)
    field, blocks = pl.pallas_call(
        functools.partial(main_kernel, nx, ny, nz),
        out_shape=[
            jax.ShapeDtypeStruct((BOXES + 8, POINTS), F32),
            jax.ShapeDtypeStruct(blocks_shape, BF16),
        ],
        in_specs=[smem, anywhere, anywhere, anywhere, anywhere],
        out_specs=[vmem, anywhere],
        scratch_shapes=[
            pltpu.VMEM(blocks_shape, BF16),
            pltpu.VMEM((OPS, POINTS, POINTS), BF16),
            pltpu.VMEM((1024, 1536), BF16),
            pltpu.VMEM((1024, 128), BF16),
            pltpu.VMEM((3, PAIRS), I32),
            pltpu.VMEM((LANES * SLOTS,), I32),
            pltpu.VMEM((16, 256), F32),
            pltpu.VMEM((BOXES, PAIRS), BF16),
            pltpu.VMEM((768, PAIRS), BF16),
            pltpu.VMEM((27, 4, 8, 256), F32),
            pltpu.VMEM((32, 128), I32),
            pltpu.VMEM((8, LANES * 64), F32),
            pltpu.VMEM((1, LANES * 64), I32),
            pltpu.VMEM((768, POINTS), BF16),
            pltpu.VMEM((LANES * 64, POINTS), BF16),
            pltpu.VMEM((1024, POINTS), F32),
            pltpu.VMEM((1024, POINTS), F32),
            pltpu.SemaphoreType.DMA((5,)),
            pltpu.SemaphoreType.DMA((52,)),
            pltpu.SemaphoreType.DMA((2, 27)),
        ],
        compiler_params=pltpu.CompilerParams(
            collective_id=0, has_side_effects=True, vmem_limit_bytes=58 * 1024 * 1024
        ),
        name="exchange",
    )(pair_count, pairs, send_list, multipoles, operators)
    return pl.pallas_call(
        remainder_kernel,
        out_shape=jax.ShapeDtypeStruct((BOXES, POINTS), F32),
        in_specs=[anywhere] * 3,
        out_specs=anywhere,
        scratch_shapes=[
            pltpu.VMEM((BOXES + 8, POINTS), F32),
            pltpu.VMEM(blocks_shape, BF16),
            pltpu.VMEM((OPS, POINTS, POINTS), BF16),
            pltpu.VMEM((27, 4, 8, 256), F32),
            pltpu.VMEM((32, 128), I32),
            pltpu.SMEM((32, 128), I32),
            pltpu.VMEM((1024, POINTS), F32),
            pltpu.SemaphoreType.DMA((4,)),
        ],
        compiler_params=pltpu.CompilerParams(vmem_limit_bytes=58 * 1024 * 1024),
        name="remainder",
    )(field, blocks, operators)


def solution(mesh):
    shape = dict(mesh.shape)
    ny = min(8, shape["gx"] // 2)
    sizes = (shape["gy"], ny, shape["gx"] // ny)
    return jax.shard_map(
        functools.partial(local, sizes),
        mesh=mesh,
        in_specs=(
            P(("gx", "gy"), None),
            P(),
            P(None, ("gx", "gy")),
            P(("gx", "gy")),
            P(("gx", "gy")),
        ),
        out_specs=P(("gx", "gy"), None),
        check_vma=False,
    )
```

```python
import functools

import jax
import jax.numpy as jnp
from jax import lax
from jax.experimental import pallas as pl
from jax.experimental.pallas import tpu as pltpu
from jax.sharding import PartitionSpec as P

MESH = pl.DeviceIdType.MESH
F32 = jnp.float32
BF16 = jnp.bfloat16
I32 = jnp.int32

BOXES = 64
POINTS = 256
PAIRS = 1024
LANES = 26
SLOTS = 24
OPS = 16
OWN = 13
ROWS = 80
WINDOW = 64


EARLY = [1, 4, 7, 10, 15, 18, 21, 24]
MIDDLE = [12, 13, 9, 11, 14, 16, 3, 5, 20, 22]
CORNERS = [0, 2, 6, 8, 17, 19, 23, 25]
ORDER = EARLY + MIDDLE + CORNERS
MID, LATE = 64 * len(EARLY), 64 * len(EARLY + MIDDLE)


def quads(lanes):
    return [lanes[i:i + 4] for i in range(0, len(lanes), 4)]


def ghost_row(lane):
    return BOXES + SLOTS * ORDER.index(lane) + (16 if lane in CORNERS else 0)


def code_of(lane):
    return lane if lane < OWN else lane + 1


def heading(code):
    return code // 9 - 1, code // 3 % 3 - 1, code % 3 - 1


def iota(shape, axis):
    return lax.broadcasted_iota(I32, shape, axis)


def one_hot(condition):
    return jnp.where(condition, 1.0, 0.0).astype(BF16)


def nt(a, b):
    return lax.dot_general(a, b, (((1,), (1,)), ((), ())), preferred_element_type=F32)


def mm(a, b):
    return jnp.dot(a, b, preferred_element_type=F32)


def pack_pairs(count, pairs_ref, send_ref, tail, meta):
    source = pairs_ref[0:1, :]
    target = pairs_ref[1:2, :]
    operator = pairs_ref[2:3, :]
    used = iota((1, PAIRS), 1) < count
    ghost = jnp.maximum(source - BOXES, 0)
    lane = jnp.right_shift(ghost * 2731, 16)
    slot = ghost - lane * SLOTS
    lane = jnp.where(used, jnp.where(source < BOXES, LANES, lane), 31)
    codes = iota((32, PAIRS), 0)
    start = jnp.sum(jnp.where(lane < codes, 1.0, 0.0), axis=1, keepdims=True)
    before = one_hot(iota((128, 128), 0) < iota((128, 128), 1))
    carry = start
    places = []
    for chunk in range(PAIRS // 128):
        hot = jnp.where(codes[:, :128] == lane[:, chunk * 128:(chunk + 1) * 128], 1.0, 0.0)
        rank = mm(hot.astype(BF16), before) + carry
        places.append(jnp.sum(hot * rank, axis=0, keepdims=True))
        carry = carry + jnp.sum(hot, axis=1, keepdims=True)
    place = jnp.concatenate(places, axis=1).astype(I32)
    fields = jnp.concatenate(
        [slot, target, operator, jnp.zeros((5, PAIRS), I32)], axis=0
    ).astype(F32).astype(BF16)
    for q in range(4):
        hot = one_hot(iota((256, PAIRS), 0) + 256 * q == place)
        ordered = nt(fields, hot)
        meta[4 * q:4 * q + 3, :] = ordered[0:3, :]
    sends = send_ref[...].reshape(1, LANES * SLOTS).astype(F32)
    meta[3:4, :] = sends[:, 0:256]
    meta[7:8, :] = sends[:, 256:512]
    meta[11:12, 0:112] = sends[:, 512:624]
    meta[11:12, 112:256] = jnp.zeros((1, 144), F32)
    diagonal = iota((32, 128), 0) == iota((32, 128), 1)
    starts = jnp.sum(jnp.where(diagonal, start, 0.0), axis=0, keepdims=True).astype(I32)
    high = jnp.right_shift(starts, 5)
    meta[15:16, 0:128] = high.astype(F32)
    meta[15:16, 128:256] = (starts - high * 32).astype(F32)
    tail[...] = meta[...].astype(BF16)


def split(value):
    high = value.astype(BF16)
    return high, (value - high.astype(F32)).astype(BF16)


def count_own(count, pairs_ref, own_counts, hot_t):
    source = pairs_ref[0:1, :]
    target = pairs_ref[1:2, :]
    operator = pairs_ref[2:3, :]
    used = jnp.logical_and(iota((1, PAIRS), 1) < count, source < BOXES)
    key = jnp.where(used, operator * BOXES + source, -1)
    hot_t[...] = one_hot(iota((BOXES, PAIRS), 0) == target)
    for q in range(4):
        hot = one_hot(iota((256, PAIRS), 0) + 256 * q == key)
        high, low = split(nt(hot, hot_t[...]))
        own_counts[256 * q:256 * (q + 1), :] = jnp.concatenate([high, low], axis=1)


def count_forward(count, pairs_ref, counts, hot_u):
    source = pairs_ref[0:1, :]
    target = pairs_ref[1:2, :]
    operator = pairs_ref[2:3, :]
    used = iota((1, PAIRS), 1) < count
    key = jnp.where(used, operator * BOXES + target, -1)
    move = jnp.zeros((1, PAIRS), I32)
    for lane in range(LANES):
        first = BOXES + SLOTS * lane
        move = jnp.where(source >= first, ghost_row(lane) - first, move)
    hot_u[...] = one_hot(iota((768, PAIRS), 0) == source + move)
    for q in range(4):
        hot = one_hot(iota((256, PAIRS), 0) + 256 * q == key)
        for c in range(3):
            high, low = split(nt(hot, hot_u[256 * c:256 * (c + 1), :]))
            counts[256 * q:256 * (q + 1), 256 * c:256 * (c + 1)] = high
            counts[256 * q:256 * (q + 1), 768 + 256 * c:768 + 256 * (c + 1)] = low


def column(row):
    n = row.shape[1]
    parts = []
    for c in range(n // 128):
        piece = jnp.broadcast_to(row[:, c * 128:(c + 1) * 128], (8, 128))
        parts.append(jnp.transpose(piece)[:, 0:1])
    return jnp.concatenate(parts, axis=0)


def unpack(blocks, code, meta, starts_v):
    wide = blocks[code, BOXES:ROWS, :].astype(F32)
    for q in range(4):
        meta[code, q, 0:4, :] = wide[4 * q:4 * q + 4, :]
        meta[code, q, 4:8, :] = wide[4 * q:4 * q + 4, :]
    starts_v[code:code + 1, :] = (wide[15:16, 0:128] * 32.0 + wide[15:16, 128:256]).astype(I32)


def longest_lane(starts):
    lengths = pltpu.roll(starts, 127, 1) - starts
    code = iota((32, 128), 0)
    back = LANES - 1 - jnp.where(code < OWN, code, code - 1)
    theirs = jnp.logical_and(iota((32, 128), 1) == back, jnp.logical_and(code != OWN, code < 27))
    lengths = jnp.where(theirs, lengths, 0).astype(F32)
    return jnp.max(jnp.max(lengths, axis=0, keepdims=True), axis=1, keepdims=True)


def window(meta, code, begin, offset):
    begin = jnp.minimum(begin, PAIRS - 1)
    chunk = lax.div(begin, 128)
    after = jnp.minimum(chunk + 1, 7)

    def piece(c):
        return meta[code, lax.div(c, 2), :, pl.ds(pl.multiple_of(lax.rem(c, 2) * 128, 128), 128)]

    shift = begin - chunk * 128
    turn = lax.rem(256 + offset - shift, 128)
    first = pltpu.roll(piece(chunk), turn, 1)
    second = pltpu.roll(piece(after), turn, 1)
    return jnp.where(iota((8, 128), 1) < 128 - shift + offset, first, second)


def gather_ghosts(blocks, group, meta, ghost):
    width = 64 * len(group)
    table = jnp.concatenate([blocks[code_of(lane), 0:BOXES, :] for lane in group], axis=0)
    picks = []
    for i, lane in enumerate(group):
        low = lane * SLOTS
        q, at = low // 128, low % 128
        cells = [meta[code_of(lane), p // 2, 3:4, p % 2 * 128:p % 2 * 128 + 128] for p in (q, min(q + 1, 5))]
        both = column(jnp.concatenate(cells, axis=1))
        picked = both[at:at + SLOTS, :].astype(I32) + 64 * i
        picks.append(jnp.where(iota((SLOTS, width), 1) == picked, 1.0, 0.0))
    hot = jnp.concatenate(picks, axis=0).astype(BF16)
    first = ghost_row(group[0])
    ghost[first:first + SLOTS * len(group), :] = mm(hot, table).astype(BF16)


def gather_events(blocks, lanes, meta, starts_v, own_boxes, events, keys_m, rows_m):
    base = 64 * ORDER.index(lanes[0])
    pairs = [lanes[i:i + 2] for i in range(0, len(lanes), 2)]
    across = iota((8 * len(pairs), 128), 1)
    upper = iota((8, 128), 0) < 4

    def stack(of_lane):
        return jnp.concatenate(
            [jnp.where(upper, of_lane(first), of_lane(second)) for first, second in pairs], axis=0
        )

    def start_of(lane, after):
        code, back = code_of(lane), LANES - 1 - lane + after
        return starts_v[code:code + 1, back:back + 1]

    begin = jnp.minimum(stack(lambda lane: start_of(lane, 0)), PAIRS - 1)
    offset = jnp.where(jnp.bitwise_and(iota(across.shape, 0), 4) == 0, 0, 64)
    chunk = jnp.right_shift(begin, 7)
    shift = begin - chunk * 128
    chunks = [
        stack(lambda lane: meta[code_of(lane), p // 2, :, p % 2 * 128:p % 2 * 128 + 128]) for p in range(8)
    ]
    now, later = chunks[0], chunks[1]
    for p in range(1, 8):
        here = chunk == p
        now = jnp.where(here, chunks[p], now)
        later = jnp.where(here, chunks[min(p + 1, 7)], later)
    amount = jnp.bitwise_and(shift - offset + 128, 127)
    for bit in range(7):
        turned = jnp.bitwise_and(amount, 1 << bit) != 0
        now = jnp.where(turned, pltpu.roll(now, 128 - (1 << bit), 1), now)
        later = jnp.where(turned, pltpu.roll(later, 128 - (1 << bit), 1), later)
    part = jnp.where(across < 128 - shift + offset, now, later)
    flat = iota((1, 128), 1)
    for i, (first, second) in enumerate(pairs):
        fields = part[8 * i:8 * i + 8, :]
        fields = jnp.where(flat < 64, fields, jnp.concatenate([fields[4:8, :], fields[0:4, :]], axis=0))
        hot = iota((SLOTS, 128), 0) == fields[0:1, :].astype(I32)
        theirs = [own_boxes[(LANES - 1 - lane) * SLOTS:(LANES - lane) * SLOTS, :] for lane in (first, second)]
        theirs = jnp.where(iota((SLOTS, 128), 1) < 64, *theirs)
        box = jnp.sum(jnp.where(hot, theirs, 0.0), axis=0, keepdims=True)
        key = (fields[2:3, :] * BOXES + box).astype(I32)
        lengths = [start_of(lane, 1) - start_of(lane, 0) for lane in (first, second)]
        key = jnp.where(jnp.where(flat < 64, flat, flat - 64) < jnp.where(flat < 64, *lengths), key, -1)
        span = slice(base + i * 128, base + (i + 1) * 128)
        events[:, span] = fields
        keys_m[0:1, span] = key
    for group in quads(lanes):
        low = 64 * ORDER.index(group[0])
        width = 64 * len(group)
        table = jnp.concatenate([blocks[code_of(lane), 0:BOXES, :] for lane in group], axis=0)
        targets = column(events[1:2, low:low + width]).astype(I32)
        which = jnp.right_shift(iota((width, 1), 0), 6)
        hot = one_hot(iota((width, width), 1) == targets + 64 * which)
        rows_m[low:low + width, :] = mm(hot, table).astype(BF16)


def apply_operators(total, forward, mirror, ops_ref, q):
    if forward is not None:
        f_high, f_low = split(forward)
    m_high, m_low = split(mirror)
    for i in range(4):
        part = slice(64 * i, 64 * i + 64)
        matrix = ops_ref[4 * q + i]
        if forward is not None:
            total += mm(jnp.concatenate([f_high[part], f_low[part]], axis=0), matrix)
        total += nt(jnp.concatenate([m_high[part], m_low[part]], axis=0), matrix)
    return total


def remainder_kernel(field_hbm, blocks_hbm, ops_hbm, out_hbm, field, blocks, ops_ref, meta, starts_v, starts_s, zm, sem):
    fetch = pltpu.make_async_copy(field_hbm, field, sem.at[0])
    fetch.start()
    fetch.wait()

    @pl.when(jnp.max(field[BOXES:, :]) > WINDOW)
    def _():
        loads = [
            pltpu.make_async_copy(blocks_hbm, blocks, sem.at[1]),
            pltpu.make_async_copy(ops_hbm, ops_ref, sem.at[2]),
        ]
        for load in loads:
            load.start()
        for load in loads:
            load.wait()
        for code in range(27):
            unpack(blocks, code, meta, starts_v)
        copy = pltpu.make_async_copy(starts_v, starts_s, sem.at[3])
        copy.start()
        copy.wait()
        own_boxes = column(jnp.concatenate([meta[OWN, q, 3:4, :] for q in range(3)], axis=1))
        zm[...] = jnp.zeros_like(zm)

        @pl.loop(0, LANES)
        def _(lane):
            code = jnp.where(lane < OWN, lane, lane + 1)
            back = LANES - 1 - lane
            begin = starts_s[code, back]
            length = starts_s[code, back + 1] - begin

            @pl.loop(1, lax.div(length + WINDOW - 1, WINDOW))
            def _(turn):
                part = window(meta, code, begin + turn * WINDOW, 0)
                boxes_row = jnp.zeros((1, 128), F32)
                slots = part[0:1, :].astype(I32) + back * SLOTS
                for q in range(6):
                    hot = iota((128, 128), 0) + 128 * q == slots
                    spread = own_boxes[q * 128:(q + 1) * 128, :]
                    boxes_row += jnp.sum(jnp.where(hot, spread, 0.0), axis=0, keepdims=True)
                key = (part[2:3, :] * BOXES + boxes_row).astype(I32)
                key = jnp.where(iota((1, 128), 1) < jnp.minimum(length - turn * WINDOW, WINDOW), key, -1)
                hot = one_hot(iota((128, BOXES), 1) == column(part[1:2, :]).astype(I32))
                rows = mm(hot, blocks[code, 0:BOXES, :]).astype(BF16)
                for q in range(4):
                    hot = one_hot(iota((256, 128), 0) + 256 * q == key)
                    zm[256 * q:256 * (q + 1), :] += mm(hot, rows)

        total = jnp.zeros((128, POINTS), F32)
        for q in range(4):
            total = apply_operators(total, None, zm[256 * q:256 * (q + 1), :], ops_ref, q)
        field[0:BOXES, :] += total[0:BOXES, :] + total[BOXES:, :]

    store = pltpu.make_async_copy(field.at[pl.ds(0, BOXES)], out_hbm, sem.at[0])
    store.start()
    store.wait()


def main_kernel(
    nx, ny, nz, count_ref, pairs_hbm, send_hbm, m_hbm, ops_hbm,
    field_ref, blocks_hbm,
    blocks, ops_ref, counts, own_counts, pairs_ref, send_ref, tail, hot_t, hot_u,
    meta, starts_v, events, keys_m, ghost, rows_m, zf, zm,
    in_sem, send_sem, recv_sem,
):
    g = lax.axis_index("gx")
    h = lax.axis_index("gy")
    by = lax.rem(g, ny)
    bz = lax.div(g, ny)
    steps = {
        "z": {1: bz < nz - 1, -1: bz > 0, 0: True},
        "y": {1: by < ny - 1, -1: by > 0, 0: True},
        "x": {1: h < nx - 1, -1: h > 0, 0: True},
    }
    partner = {
        "z": lambda s: (g + s * ny, h),
        "y": lambda s: (g + s, h),
        "x": lambda s: (g, h + s),
    }

    def on_grid(dx, dy, dz):
        cond = None
        for flag in (steps["x"][dx], steps["y"][dy], steps["z"][dz]):
            if flag is not True:
                cond = flag if cond is None else jnp.logical_and(cond, flag)
        return cond

    barrier = pltpu.get_barrier_semaphore()
    for axis in "zyx":
        for s in (1, -1):
            @pl.when(steps[axis][s])
            def _():
                pl.semaphore_signal(barrier, inc=1, device_id=partner[axis](s), device_id_type=MESH)

    loads = [
        pltpu.make_async_copy(src, dst, in_sem.at[i])
        for i, (src, dst) in enumerate([
            (pairs_hbm, pairs_ref),
            (send_hbm, send_ref),
            (m_hbm, blocks.at[OWN, pl.ds(0, BOXES)]),
            (ops_hbm, ops_ref),
        ])
    ]
    for load in loads:
        load.start()

    def as_code(dx, dy, dz):
        return (dx + 1) * 9 + (dy + 1) * 3 + dz + 1

    spans = [pl.ds(0, ROWS)]
    started = []

    def send(src, axis, s, part):
        dx, dy, dz = src
        dst = {"x": (-s, dy, dz), "y": (dx, -s, dz), "z": (dx, dy, -s)}[axis]
        need = {"x": (s, dy, dz), "y": (dx, s, dz), "z": (dx, dy, s)}[axis]
        cond = on_grid(*need)
        own = False
        copy = pltpu.make_async_remote_copy(
            src_ref=m_hbm if own else blocks.at[as_code(*src), spans[part]],
            dst_ref=blocks.at[as_code(*dst), spans[part]],
            send_sem=send_sem.at[len(started)],
            recv_sem=recv_sem.at[part, as_code(*dst)],
            device_id=partner[axis](s),
            device_id_type=MESH,
        )
        started.append((copy, cond))
        pl.when(cond)(copy.start)

    def arrived(where, part):
        code = as_code(*where)
        slot = blocks.at[code, spans[part]]
        copy = pltpu.make_async_remote_copy(
            src_ref=slot, dst_ref=slot, send_sem=send_sem.at[0], recv_sem=recv_sem.at[part, code],
            device_id=(g, h), device_id_type=MESH,
        )
        pl.when(on_grid(*where))(copy.wait_recv)

    def send_home(part):
        for axis in "zyx":
            for s in (1, -1):
                send((0, 0, 0), axis, s, part)

    def relay(places, axes, part):
        for where in places:
            arrived(where, part)
            for axis in axes:
                for s in (1, -1):
                    send(where, axis, s, part)

    along_y = [(0, 1, 0), (0, -1, 0)]
    along_z = [(0, 0, 1), (0, 0, -1)]
    along_yz = [(0, 1, 1), (0, -1, 1), (0, 1, -1), (0, -1, -1)]
    count = count_ref[0]
    loads[0].wait()
    loads[1].wait()
    pack_pairs(count, pairs_ref, send_ref, blocks.at[OWN, pl.ds(BOXES, ROWS - BOXES)], tail)
    loads[2].wait()
    pl.semaphore_wait(
        barrier,
        sum(steps[axis][s].astype(I32) for axis in "zyx" for s in (1, -1)),
    )
    send_home(0)
    for code in range(27):
        if code != OWN:
            @pl.when(jnp.logical_not(on_grid(*heading(code))))
            def _():
                blocks[code] = jnp.zeros((ROWS, POINTS), BF16)
    starts_v[27:32, :] = jnp.zeros((5, 128), I32)
    ghost[496:512, :] = jnp.zeros((16, POINTS), BF16)
    ghost[704:768, :] = jnp.zeros((64, POINTS), BF16)
    own_boxes = column(
        jnp.concatenate([tail[4 * q + 3:4 * q + 4, :] for q in range(3)], axis=1)
    )
    count_own(count, pairs_ref, own_counts, hot_t)
    count_forward(count, pairs_ref, counts, hot_u)
    relay(along_y, "x", 0)
    relay(along_z, "yx", 0)
    loads[3].wait()

    def take(lanes):
        for lane in lanes:
            unpack(blocks, code_of(lane), meta, starts_v)
        for group in quads(lanes):
            gather_ghosts(blocks, group, meta, ghost)
        gather_events(blocks, lanes, meta, starts_v, own_boxes, events, keys_m, rows_m)

    def wait_for(lanes):
        for lane in lanes:
            if heading(code_of(lane))[0] != 0:
                arrived(heading(code_of(lane)), 0)

    def sums(q, low, high, first, last):
        span = slice(256 * q, 256 * (q + 1))
        forward = mm(counts[span, low:high], ghost[low:high, :])
        forward += mm(counts[span, 768 + low:768 + high], ghost[low:high, :])
        hot = one_hot(iota((256, last - first), 0) + 256 * q == keys_m[:, first:last])
        return forward, mm(hot, rows_m[first:last, :])

    ghost[0:BOXES, :] = blocks[OWN, 0:BOXES, :]
    starts_v[0:27, :] = jnp.zeros((27, 128), I32)
    wait_for(EARLY)
    take(EARLY)
    own = blocks[OWN, 0:BOXES, :]
    own_twice = jnp.concatenate([own, own], axis=0)
    quarters = [slice(256 * q, 256 * (q + 1)) for q in range(4)]
    for q, span in enumerate(quarters):
        forward, mirror = sums(q, 0, 256, 0, MID)
        zf[span, :] = forward
        zm[span, :] = mirror + mm(own_counts[span, :], own_twice)

    relay(along_yz, "x", 0)
    wait_for(MIDDLE)
    take(MIDDLE)
    for q, span in enumerate(quarters):
        forward, mirror = sums(q, 256, 512, MID, LATE)
        zf[span, :] += forward
        zm[span, :] += mirror

    wait_for(CORNERS)
    save = pltpu.make_async_copy(blocks, blocks_hbm, in_sem.at[4])
    save.start()
    take(CORNERS)
    total = jnp.zeros((128, POINTS), F32)
    for q, span in enumerate(quarters):
        forward, mirror = sums(q, 512, 768, LATE, 64 * LANES)
        total = apply_operators(total, zf[span, :] + forward, zm[span, :] + mirror, ops_ref, q)
    field_ref[0:BOXES, :] = total[0:BOXES, :] + total[BOXES:, :]
    field_ref[BOXES:, :] = jnp.full((8, POINTS), 0.0, F32) + longest_lane(starts_v[...])
    save.wait()
    for copy, cond in started:
        pl.when(cond)(copy.wait_send)


def local(sizes, multipoles, operators, pairs, pair_count, send_list):
    nx, ny, nz = sizes
    smem = pl.BlockSpec(memory_space=pltpu.SMEM)
    vmem = pl.BlockSpec(memory_space=pltpu.VMEM)
    anywhere = pl.BlockSpec(memory_space=pl.ANY)
    blocks_shape = (27, ROWS, POINTS)
    field, blocks = pl.pallas_call(
        functools.partial(main_kernel, nx, ny, nz),
        out_shape=[
            jax.ShapeDtypeStruct((BOXES + 8, POINTS), F32),
            jax.ShapeDtypeStruct(blocks_shape, BF16),
        ],
        in_specs=[smem, anywhere, anywhere, anywhere, anywhere],
        out_specs=[vmem, anywhere],
        scratch_shapes=[
            pltpu.VMEM(blocks_shape, BF16),
            pltpu.VMEM((OPS, POINTS, POINTS), BF16),
            pltpu.VMEM((1024, 1536), BF16),
            pltpu.VMEM((1024, 128), BF16),
            pltpu.VMEM((3, PAIRS), I32),
            pltpu.VMEM((LANES * SLOTS,), I32),
            pltpu.VMEM((16, 256), F32),
            pltpu.VMEM((BOXES, PAIRS), BF16),
            pltpu.VMEM((768, PAIRS), BF16),
            pltpu.VMEM((27, 4, 8, 256), F32),
            pltpu.VMEM((32, 128), I32),
            pltpu.VMEM((8, LANES * 64), F32),
            pltpu.VMEM((1, LANES * 64), I32),
            pltpu.VMEM((768, POINTS), BF16),
            pltpu.VMEM((LANES * 64, POINTS), BF16),
            pltpu.VMEM((1024, POINTS), F32),
            pltpu.VMEM((1024, POINTS), F32),
            pltpu.SemaphoreType.DMA((5,)),
            pltpu.SemaphoreType.DMA((52,)),
            pltpu.SemaphoreType.DMA((2, 27)),
        ],
        compiler_params=pltpu.CompilerParams(
            collective_id=0, has_side_effects=True, vmem_limit_bytes=58 * 1024 * 1024
        ),
        name="exchange",
    )(pair_count, pairs, send_list, multipoles, operators)
    return pl.pallas_call(
        remainder_kernel,
        out_shape=jax.ShapeDtypeStruct((BOXES, POINTS), F32),
        in_specs=[anywhere] * 3,
        out_specs=anywhere,
        scratch_shapes=[
            pltpu.VMEM((BOXES + 8, POINTS), F32),
            pltpu.VMEM(blocks_shape, BF16),
            pltpu.VMEM((OPS, POINTS, POINTS), BF16),
            pltpu.VMEM((27, 4, 8, 256), F32),
            pltpu.VMEM((32, 128), I32),
            pltpu.SMEM((32, 128), I32),
            pltpu.VMEM((1024, POINTS), F32),
            pltpu.SemaphoreType.DMA((4,)),
        ],
        compiler_params=pltpu.CompilerParams(vmem_limit_bytes=58 * 1024 * 1024),
        name="remainder",
    )(field, blocks, operators)


def solution(mesh):
    shape = dict(mesh.shape)
    ny = min(8, shape["gx"] // 2)
    sizes = (shape["gy"], ny, shape["gx"] // ny)
    return jax.shard_map(
        functools.partial(local, sizes),
        mesh=mesh,
        in_specs=(
            P(("gx", "gy"), None),
            P(),
            P(None, ("gx", "gy")),
            P(("gx", "gy")),
            P(("gx", "gy")),
        ),
        out_specs=P(("gx", "gy"), None),
        check_vma=False,
    )
```

```python
import functools

import jax
import jax.numpy as jnp
from jax import lax
from jax.experimental import pallas as pl
from jax.experimental.pallas import tpu as pltpu
from jax.sharding import PartitionSpec as P

MESH = pl.DeviceIdType.MESH
F32 = jnp.float32
BF16 = jnp.bfloat16
I32 = jnp.int32

BOXES = 64
POINTS = 256
PAIRS = 1024
LANES = 26
SLOTS = 24
OPS = 16
OWN = 13
ROWS = 80
WINDOW = 64


EARLY = [1, 4, 7, 10, 15, 18, 21, 24]
MIDDLE = [12, 13, 9, 11, 14, 16, 3, 5, 20, 22]
CORNERS = [0, 2, 6, 8, 17, 19, 23, 25]
ORDER = EARLY + MIDDLE + CORNERS
MID, LATE = 64 * len(EARLY), 64 * len(EARLY + MIDDLE)


def quads(lanes):
    return [lanes[i:i + 4] for i in range(0, len(lanes), 4)]


def ghost_row(lane):
    return BOXES + SLOTS * ORDER.index(lane) + (16 if lane in CORNERS else 0)


def code_of(lane):
    return lane if lane < OWN else lane + 1


def heading(code):
    return code // 9 - 1, code // 3 % 3 - 1, code % 3 - 1


def iota(shape, axis):
    return lax.broadcasted_iota(I32, shape, axis)


def one_hot(condition):
    return jnp.where(condition, 1.0, 0.0).astype(BF16)


def nt(a, b):
    return lax.dot_general(a, b, (((1,), (1,)), ((), ())), preferred_element_type=F32)


def mm(a, b):
    return jnp.dot(a, b, preferred_element_type=F32)


def pack_pairs(count, pairs_ref, send_ref, tail, meta):
    source = pairs_ref[0:1, :]
    target = pairs_ref[1:2, :]
    operator = pairs_ref[2:3, :]
    used = iota((1, PAIRS), 1) < count
    ghost = jnp.maximum(source - BOXES, 0)
    lane = jnp.right_shift(ghost * 2731, 16)
    slot = ghost - lane * SLOTS
    lane = jnp.where(used, jnp.where(source < BOXES, LANES, lane), 31)
    codes = iota((32, PAIRS), 0)
    start = jnp.sum(jnp.where(lane < codes, 1.0, 0.0), axis=1, keepdims=True)
    before = one_hot(iota((128, 128), 0) < iota((128, 128), 1))
    carry = start
    places = []
    for chunk in range(PAIRS // 128):
        hot = jnp.where(codes[:, :128] == lane[:, chunk * 128:(chunk + 1) * 128], 1.0, 0.0)
        rank = mm(hot.astype(BF16), before) + carry
        places.append(jnp.sum(hot * rank, axis=0, keepdims=True))
        carry = carry + jnp.sum(hot, axis=1, keepdims=True)
    place = jnp.concatenate(places, axis=1).astype(I32)
    fields = jnp.concatenate(
        [slot, target, operator, jnp.zeros((5, PAIRS), I32)], axis=0
    ).astype(F32).astype(BF16)
    for q in range(4):
        hot = one_hot(iota((256, PAIRS), 0) + 256 * q == place)
        ordered = nt(fields, hot)
        meta[4 * q:4 * q + 3, :] = ordered[0:3, :]
    sends = send_ref[...].reshape(1, LANES * SLOTS).astype(F32)
    meta[3:4, :] = sends[:, 0:256]
    meta[7:8, :] = sends[:, 256:512]
    meta[11:12, 0:112] = sends[:, 512:624]
    meta[11:12, 112:256] = jnp.zeros((1, 144), F32)
    diagonal = iota((32, 128), 0) == iota((32, 128), 1)
    starts = jnp.sum(jnp.where(diagonal, start, 0.0), axis=0, keepdims=True).astype(I32)
    high = jnp.right_shift(starts, 5)
    meta[15:16, 0:128] = high.astype(F32)
    meta[15:16, 128:256] = (starts - high * 32).astype(F32)
    tail[...] = meta[...].astype(BF16)


def split(value):
    high = value.astype(BF16)
    return high, (value - high.astype(F32)).astype(BF16)


def count_own(count, pairs_ref, own_counts, hot_t):
    source = pairs_ref[0:1, :]
    target = pairs_ref[1:2, :]
    operator = pairs_ref[2:3, :]
    used = jnp.logical_and(iota((1, PAIRS), 1) < count, source < BOXES)
    key = jnp.where(used, operator * BOXES + source, -1)
    hot_t[...] = one_hot(iota((BOXES, PAIRS), 0) == target)
    for q in range(4):
        hot = one_hot(iota((256, PAIRS), 0) + 256 * q == key)
        high, low = split(nt(hot, hot_t[...]))
        own_counts[256 * q:256 * (q + 1), :] = jnp.concatenate([high, low], axis=1)


def count_forward(count, pairs_ref, counts, hot_u):
    source = pairs_ref[0:1, :]
    target = pairs_ref[1:2, :]
    operator = pairs_ref[2:3, :]
    used = iota((1, PAIRS), 1) < count
    key = jnp.where(used, operator * BOXES + target, -1)
    move = jnp.zeros((1, PAIRS), I32)
    for lane in range(LANES):
        first = BOXES + SLOTS * lane
        move = jnp.where(source >= first, ghost_row(lane) - first, move)
    hot_u[...] = one_hot(iota((768, PAIRS), 0) == source + move)
    for q in range(4):
        hot = one_hot(iota((256, PAIRS), 0) + 256 * q == key)
        for c in range(3):
            high, low = split(nt(hot, hot_u[256 * c:256 * (c + 1), :]))
            counts[256 * q:256 * (q + 1), 256 * c:256 * (c + 1)] = high
            counts[256 * q:256 * (q + 1), 768 + 256 * c:768 + 256 * (c + 1)] = low


def column(row):
    n = row.shape[1]
    parts = []
    for c in range(n // 128):
        piece = jnp.broadcast_to(row[:, c * 128:(c + 1) * 128], (8, 128))
        parts.append(jnp.transpose(piece)[:, 0:1])
    return jnp.concatenate(parts, axis=0)


def unpack(blocks, code, meta, starts_v):
    wide = blocks[code, BOXES:ROWS, :].astype(F32)
    for q in range(4):
        meta[code, q, 0:4, :] = wide[4 * q:4 * q + 4, :]
        meta[code, q, 4:8, :] = wide[4 * q:4 * q + 4, :]
    starts_v[code:code + 1, :] = (wide[15:16, 0:128] * 32.0 + wide[15:16, 128:256]).astype(I32)


def longest_lane(starts):
    lengths = pltpu.roll(starts, 127, 1) - starts
    code = iota((32, 128), 0)
    back = LANES - 1 - jnp.where(code < OWN, code, code - 1)
    theirs = jnp.logical_and(iota((32, 128), 1) == back, jnp.logical_and(code != OWN, code < 27))
    lengths = jnp.where(theirs, lengths, 0).astype(F32)
    return jnp.max(jnp.max(lengths, axis=0, keepdims=True), axis=1, keepdims=True)


def window(meta, code, begin, offset):
    begin = jnp.minimum(begin, PAIRS - 1)
    chunk = lax.div(begin, 128)
    after = jnp.minimum(chunk + 1, 7)

    def piece(c):
        return meta[code, lax.div(c, 2), :, pl.ds(pl.multiple_of(lax.rem(c, 2) * 128, 128), 128)]

    shift = begin - chunk * 128
    turn = lax.rem(256 + offset - shift, 128)
    first = pltpu.roll(piece(chunk), turn, 1)
    second = pltpu.roll(piece(after), turn, 1)
    return jnp.where(iota((8, 128), 1) < 128 - shift + offset, first, second)


def gather_ghosts(blocks, group, meta, ghost):
    width = 64 * len(group)
    table = jnp.concatenate([blocks[code_of(lane), 0:BOXES, :] for lane in group], axis=0)
    picks = []
    for i, lane in enumerate(group):
        low = lane * SLOTS
        q, at = low // 128, low % 128
        cells = [meta[code_of(lane), p // 2, 3:4, p % 2 * 128:p % 2 * 128 + 128] for p in (q, min(q + 1, 5))]
        both = column(jnp.concatenate(cells, axis=1))
        picked = both[at:at + SLOTS, :].astype(I32) + 64 * i
        picks.append(jnp.where(iota((SLOTS, width), 1) == picked, 1.0, 0.0))
    hot = jnp.concatenate(picks, axis=0).astype(BF16)
    first = ghost_row(group[0])
    ghost[first:first + SLOTS * len(group), :] = mm(hot, table).astype(BF16)


def gather_events(blocks, lanes, meta, starts_v, own_boxes, events, keys_m, rows_m):
    base = 64 * ORDER.index(lanes[0])
    pairs = [lanes[i:i + 2] for i in range(0, len(lanes), 2)]
    across = iota((8 * len(pairs), 128), 1)
    upper = iota((8, 128), 0) < 4

    def stack(of_lane):
        return jnp.concatenate(
            [jnp.where(upper, of_lane(first), of_lane(second)) for first, second in pairs], axis=0
        )

    def start_of(lane, after):
        code, back = code_of(lane), LANES - 1 - lane + after
        return starts_v[code:code + 1, back:back + 1]

    begin = jnp.minimum(stack(lambda lane: start_of(lane, 0)), PAIRS - 1)
    offset = jnp.where(jnp.bitwise_and(iota(across.shape, 0), 4) == 0, 0, 64)
    chunk = jnp.right_shift(begin, 7)
    shift = begin - chunk * 128
    chunks = [
        stack(lambda lane: meta[code_of(lane), p // 2, :, p % 2 * 128:p % 2 * 128 + 128]) for p in range(8)
    ]
    now, later = chunks[0], chunks[1]
    for p in range(1, 8):
        here = chunk == p
        now = jnp.where(here, chunks[p], now)
        later = jnp.where(here, chunks[min(p + 1, 7)], later)
    amount = jnp.bitwise_and(shift - offset + 128, 127)
    for bit in range(7):
        turned = jnp.bitwise_and(amount, 1 << bit) != 0
        now = jnp.where(turned, pltpu.roll(now, 128 - (1 << bit), 1), now)
        later = jnp.where(turned, pltpu.roll(later, 128 - (1 << bit), 1), later)
    part = jnp.where(across < 128 - shift + offset, now, later)
    flat = iota((1, 128), 1)
    for i, (first, second) in enumerate(pairs):
        fields = part[8 * i:8 * i + 8, :]
        fields = jnp.where(flat < 64, fields, jnp.concatenate([fields[4:8, :], fields[0:4, :]], axis=0))
        hot = iota((SLOTS, 128), 0) == fields[0:1, :].astype(I32)
        theirs = [own_boxes[(LANES - 1 - lane) * SLOTS:(LANES - lane) * SLOTS, :] for lane in (first, second)]
        theirs = jnp.where(iota((SLOTS, 128), 1) < 64, *theirs)
        box = jnp.sum(jnp.where(hot, theirs, 0.0), axis=0, keepdims=True)
        key = (fields[2:3, :] * BOXES + box).astype(I32)
        lengths = [start_of(lane, 1) - start_of(lane, 0) for lane in (first, second)]
        key = jnp.where(jnp.where(flat < 64, flat, flat - 64) < jnp.where(flat < 64, *lengths), key, -1)
        span = slice(base + i * 128, base + (i + 1) * 128)
        events[:, span] = fields
        keys_m[0:1, span] = key
    for group in quads(lanes):
        low = 64 * ORDER.index(group[0])
        width = 64 * len(group)
        table = jnp.concatenate([blocks[code_of(lane), 0:BOXES, :] for lane in group], axis=0)
        targets = column(events[1:2, low:low + width]).astype(I32)
        which = jnp.right_shift(iota((width, 1), 0), 6)
        hot = one_hot(iota((width, width), 1) == targets + 64 * which)
        rows_m[low:low + width, :] = mm(hot, table).astype(BF16)


def apply_operators(total, forward, mirror, ops_ref, q):
    if forward is not None:
        f_high, f_low = split(forward)
    m_high, m_low = split(mirror)
    for i in range(4):
        part = slice(64 * i, 64 * i + 64)
        matrix = ops_ref[4 * q + i]
        if forward is not None:
            total += mm(jnp.concatenate([f_high[part], f_low[part]], axis=0), matrix)
        total += nt(jnp.concatenate([m_high[part], m_low[part]], axis=0), matrix)
    return total


def remainder_kernel(field_hbm, blocks_hbm, ops_hbm, out_hbm, field, blocks, ops_ref, meta, starts_v, starts_s, zm, sem):
    fetch = pltpu.make_async_copy(field_hbm, field, sem.at[0])
    fetch.start()
    fetch.wait()

    @pl.when(jnp.max(field[BOXES:, :]) > WINDOW)
    def _():
        loads = [
            pltpu.make_async_copy(blocks_hbm, blocks, sem.at[1]),
            pltpu.make_async_copy(ops_hbm, ops_ref, sem.at[2]),
        ]
        for load in loads:
            load.start()
        for load in loads:
            load.wait()
        for code in range(27):
            unpack(blocks, code, meta, starts_v)
        copy = pltpu.make_async_copy(starts_v, starts_s, sem.at[3])
        copy.start()
        copy.wait()
        own_boxes = column(jnp.concatenate([meta[OWN, q, 3:4, :] for q in range(3)], axis=1))
        zm[...] = jnp.zeros_like(zm)

        @pl.loop(0, LANES)
        def _(lane):
            code = jnp.where(lane < OWN, lane, lane + 1)
            back = LANES - 1 - lane
            begin = starts_s[code, back]
            length = starts_s[code, back + 1] - begin

            @pl.loop(1, lax.div(length + WINDOW - 1, WINDOW))
            def _(turn):
                part = window(meta, code, begin + turn * WINDOW, 0)
                boxes_row = jnp.zeros((1, 128), F32)
                slots = part[0:1, :].astype(I32) + back * SLOTS
                for q in range(6):
                    hot = iota((128, 128), 0) + 128 * q == slots
                    spread = own_boxes[q * 128:(q + 1) * 128, :]
                    boxes_row += jnp.sum(jnp.where(hot, spread, 0.0), axis=0, keepdims=True)
                key = (part[2:3, :] * BOXES + boxes_row).astype(I32)
                key = jnp.where(iota((1, 128), 1) < jnp.minimum(length - turn * WINDOW, WINDOW), key, -1)
                hot = one_hot(iota((128, BOXES), 1) == column(part[1:2, :]).astype(I32))
                rows = mm(hot, blocks[code, 0:BOXES, :]).astype(BF16)
                for q in range(4):
                    hot = one_hot(iota((256, 128), 0) + 256 * q == key)
                    zm[256 * q:256 * (q + 1), :] += mm(hot, rows)

        total = jnp.zeros((128, POINTS), F32)
        for q in range(4):
            total = apply_operators(total, None, zm[256 * q:256 * (q + 1), :], ops_ref, q)
        field[0:BOXES, :] += total[0:BOXES, :] + total[BOXES:, :]

    store = pltpu.make_async_copy(field.at[pl.ds(0, BOXES)], out_hbm, sem.at[0])
    store.start()
    store.wait()


def main_kernel(
    nx, ny, nz, count_ref, pairs_hbm, send_hbm, m_hbm, ops_hbm,
    field_ref, blocks_hbm,
    blocks, ops_ref, counts, own_counts, pairs_ref, send_ref, tail, hot_t, hot_u,
    meta, starts_v, events, keys_m, ghost, rows_m, zf, zm,
    in_sem, send_sem, recv_sem,
):
    g = lax.axis_index("gx")
    h = lax.axis_index("gy")
    by = lax.rem(g, ny)
    bz = lax.div(g, ny)
    steps = {
        "z": {1: bz < nz - 1, -1: bz > 0, 0: True},
        "y": {1: by < ny - 1, -1: by > 0, 0: True},
        "x": {1: h < nx - 1, -1: h > 0, 0: True},
    }
    partner = {
        "z": lambda s: (g + s * ny, h),
        "y": lambda s: (g + s, h),
        "x": lambda s: (g, h + s),
    }

    def on_grid(dx, dy, dz):
        cond = None
        for flag in (steps["x"][dx], steps["y"][dy], steps["z"][dz]):
            if flag is not True:
                cond = flag if cond is None else jnp.logical_and(cond, flag)
        return cond

    barrier = pltpu.get_barrier_semaphore()
    for axis in "zyx":
        for s in (1, -1):
            @pl.when(steps[axis][s])
            def _():
                pl.semaphore_signal(barrier, inc=1, device_id=partner[axis](s), device_id_type=MESH)

    loads = [
        pltpu.make_async_copy(src, dst, in_sem.at[i])
        for i, (src, dst) in enumerate([
            (pairs_hbm, pairs_ref),
            (send_hbm, send_ref),
            (m_hbm, blocks.at[OWN, pl.ds(0, BOXES)]),
            (ops_hbm, ops_ref),
        ])
    ]
    for load in loads:
        load.start()

    def as_code(dx, dy, dz):
        return (dx + 1) * 9 + (dy + 1) * 3 + dz + 1

    spans = [pl.ds(0, ROWS)]
    started = []

    def send(src, axis, s, part):
        dx, dy, dz = src
        dst = {"x": (-s, dy, dz), "y": (dx, -s, dz), "z": (dx, dy, -s)}[axis]
        need = {"x": (s, dy, dz), "y": (dx, s, dz), "z": (dx, dy, s)}[axis]
        cond = on_grid(*need)
        own = False
        copy = pltpu.make_async_remote_copy(
            src_ref=m_hbm if own else blocks.at[as_code(*src), spans[part]],
            dst_ref=blocks.at[as_code(*dst), spans[part]],
            send_sem=send_sem.at[len(started)],
            recv_sem=recv_sem.at[part, as_code(*dst)],
            device_id=partner[axis](s),
            device_id_type=MESH,
        )
        started.append((copy, cond))
        pl.when(cond)(copy.start)

    def arrived(where, part):
        code = as_code(*where)
        slot = blocks.at[code, spans[part]]
        copy = pltpu.make_async_remote_copy(
            src_ref=slot, dst_ref=slot, send_sem=send_sem.at[0], recv_sem=recv_sem.at[part, code],
            device_id=(g, h), device_id_type=MESH,
        )
        pl.when(on_grid(*where))(copy.wait_recv)

    def send_home(part):
        for axis in "zyx":
            for s in (1, -1):
                send((0, 0, 0), axis, s, part)

    def relay(places, axes, part):
        for where in places:
            arrived(where, part)
            for axis in axes:
                for s in (1, -1):
                    send(where, axis, s, part)

    along_y = [(0, 1, 0), (0, -1, 0)]
    along_z = [(0, 0, 1), (0, 0, -1)]
    along_yz = [(0, 1, 1), (0, -1, 1), (0, 1, -1), (0, -1, -1)]
    count = count_ref[0]
    loads[0].wait()
    loads[1].wait()
    pack_pairs(count, pairs_ref, send_ref, blocks.at[OWN, pl.ds(BOXES, ROWS - BOXES)], tail)
    loads[2].wait()
    pl.semaphore_wait(
        barrier,
        sum(steps[axis][s].astype(I32) for axis in "zyx" for s in (1, -1)),
    )
    send_home(0)
    for code in range(27):
        if code != OWN:
            @pl.when(jnp.logical_not(on_grid(*heading(code))))
            def _():
                blocks[code] = jnp.zeros((ROWS, POINTS), BF16)
    starts_v[27:32, :] = jnp.zeros((5, 128), I32)
    ghost[496:512, :] = jnp.zeros((16, POINTS), BF16)
    ghost[704:768, :] = jnp.zeros((64, POINTS), BF16)
    own_boxes = column(
        jnp.concatenate([tail[4 * q + 3:4 * q + 4, :] for q in range(3)], axis=1)
    )
    count_own(count, pairs_ref, own_counts, hot_t)
    count_forward(count, pairs_ref, counts, hot_u)
    relay(along_y, "x", 0)
    relay(along_z, "yx", 0)
    loads[3].wait()

    def take(lanes):
        for lane in lanes:
            unpack(blocks, code_of(lane), meta, starts_v)
        for group in quads(lanes):
            gather_ghosts(blocks, group, meta, ghost)
        gather_events(blocks, lanes, meta, starts_v, own_boxes, events, keys_m, rows_m)

    def wait_for(lanes):
        for lane in lanes:
            if heading(code_of(lane))[0] != 0:
                arrived(heading(code_of(lane)), 0)

    def sums(q, low, high, first, last):
        span = slice(256 * q, 256 * (q + 1))
        forward = mm(counts[span, low:high], ghost[low:high, :])
        forward += mm(counts[span, 768 + low:768 + high], ghost[low:high, :])
        hot = one_hot(iota((256, last - first), 0) + 256 * q == keys_m[:, first:last])
        return forward, mm(hot, rows_m[first:last, :])

    ghost[0:BOXES, :] = blocks[OWN, 0:BOXES, :]
    starts_v[0:27, :] = jnp.zeros((27, 128), I32)
    wait_for(EARLY)
    take(EARLY)
    own = blocks[OWN, 0:BOXES, :]
    own_twice = jnp.concatenate([own, own], axis=0)
    quarters = [slice(256 * q, 256 * (q + 1)) for q in range(4)]
    relay(along_yz, "x", 0)
    wait_for(MIDDLE)
    take(MIDDLE)
    for q, span in enumerate(quarters):
        forward, mirror = sums(q, 0, 512, 0, LATE)
        zf[span, :] = forward
        zm[span, :] = mirror + mm(own_counts[span, :], own_twice)

    wait_for(CORNERS)
    save = pltpu.make_async_copy(blocks, blocks_hbm, in_sem.at[4])
    save.start()
    take(CORNERS)
    total = jnp.zeros((128, POINTS), F32)
    for q, span in enumerate(quarters):
        forward, mirror = sums(q, 512, 768, LATE, 64 * LANES)
        total = apply_operators(total, zf[span, :] + forward, zm[span, :] + mirror, ops_ref, q)
    field_ref[0:BOXES, :] = total[0:BOXES, :] + total[BOXES:, :]
    field_ref[BOXES:, :] = jnp.full((8, POINTS), 0.0, F32) + longest_lane(starts_v[...])
    save.wait()
    for copy, cond in started:
        pl.when(cond)(copy.wait_send)


def local(sizes, multipoles, operators, pairs, pair_count, send_list):
    nx, ny, nz = sizes
    smem = pl.BlockSpec(memory_space=pltpu.SMEM)
    vmem = pl.BlockSpec(memory_space=pltpu.VMEM)
    anywhere = pl.BlockSpec(memory_space=pl.ANY)
    blocks_shape = (27, ROWS, POINTS)
    field, blocks = pl.pallas_call(
        functools.partial(main_kernel, nx, ny, nz),
        out_shape=[
            jax.ShapeDtypeStruct((BOXES + 8, POINTS), F32),
            jax.ShapeDtypeStruct(blocks_shape, BF16),
        ],
        in_specs=[smem, anywhere, anywhere, anywhere, anywhere],
        out_specs=[vmem, anywhere],
        scratch_shapes=[
            pltpu.VMEM(blocks_shape, BF16),
            pltpu.VMEM((OPS, POINTS, POINTS), BF16),
            pltpu.VMEM((1024, 1536), BF16),
            pltpu.VMEM((1024, 128), BF16),
            pltpu.VMEM((3, PAIRS), I32),
            pltpu.VMEM((LANES * SLOTS,), I32),
            pltpu.VMEM((16, 256), F32),
            pltpu.VMEM((BOXES, PAIRS), BF16),
            pltpu.VMEM((768, PAIRS), BF16),
            pltpu.VMEM((27, 4, 8, 256), F32),
            pltpu.VMEM((32, 128), I32),
            pltpu.VMEM((8, LANES * 64), F32),
            pltpu.VMEM((1, LANES * 64), I32),
            pltpu.VMEM((768, POINTS), BF16),
            pltpu.VMEM((LANES * 64, POINTS), BF16),
            pltpu.VMEM((1024, POINTS), F32),
            pltpu.VMEM((1024, POINTS), F32),
            pltpu.SemaphoreType.DMA((5,)),
            pltpu.SemaphoreType.DMA((52,)),
            pltpu.SemaphoreType.DMA((2, 27)),
        ],
        compiler_params=pltpu.CompilerParams(
            collective_id=0, has_side_effects=True, vmem_limit_bytes=58 * 1024 * 1024
        ),
        name="exchange",
    )(pair_count, pairs, send_list, multipoles, operators)
    return pl.pallas_call(
        remainder_kernel,
        out_shape=jax.ShapeDtypeStruct((BOXES, POINTS), F32),
        in_specs=[anywhere] * 3,
        out_specs=anywhere,
        scratch_shapes=[
            pltpu.VMEM((BOXES + 8, POINTS), F32),
            pltpu.VMEM(blocks_shape, BF16),
            pltpu.VMEM((OPS, POINTS, POINTS), BF16),
            pltpu.VMEM((27, 4, 8, 256), F32),
            pltpu.VMEM((32, 128), I32),
            pltpu.SMEM((32, 128), I32),
            pltpu.VMEM((1024, POINTS), F32),
            pltpu.SemaphoreType.DMA((4,)),
        ],
        compiler_params=pltpu.CompilerParams(vmem_limit_bytes=58 * 1024 * 1024),
        name="remainder",
    )(field, blocks, operators)


def solution(mesh):
    shape = dict(mesh.shape)
    ny = min(8, shape["gx"] // 2)
    sizes = (shape["gy"], ny, shape["gx"] // ny)
    return jax.shard_map(
        functools.partial(local, sizes),
        mesh=mesh,
        in_specs=(
            P(("gx", "gy"), None),
            P(),
            P(None, ("gx", "gy")),
            P(("gx", "gy")),
            P(("gx", "gy")),
        ),
        out_specs=P(("gx", "gy"), None),
        check_vma=False,
    )
```

```python
import functools

import jax
import jax.numpy as jnp
from jax import lax
from jax.experimental import pallas as pl
from jax.experimental.pallas import tpu as pltpu
from jax.sharding import PartitionSpec as P

MESH = pl.DeviceIdType.MESH
F32 = jnp.float32
BF16 = jnp.bfloat16
I32 = jnp.int32

BOXES = 64
POINTS = 256
PAIRS = 1024
LANES = 26
SLOTS = 24
OPS = 16
OWN = 13
ROWS = 80
WINDOW = 64


EARLY = [1, 4, 7, 10, 15, 18, 21, 24]
MIDDLE = [12, 13, 9, 11, 14, 16, 3, 5, 20, 22]
CORNERS = [0, 2, 6, 8, 17, 19, 23, 25]
ORDER = EARLY + MIDDLE + CORNERS
MID, LATE = 64 * len(EARLY), 64 * len(EARLY + MIDDLE)


def quads(lanes):
    return [lanes[i:i + 4] for i in range(0, len(lanes), 4)]


def ghost_row(lane):
    return BOXES + SLOTS * ORDER.index(lane) + (16 if lane in CORNERS else 0)


def code_of(lane):
    return lane if lane < OWN else lane + 1


def heading(code):
    return code // 9 - 1, code // 3 % 3 - 1, code % 3 - 1


def iota(shape, axis):
    return lax.broadcasted_iota(I32, shape, axis)


def one_hot(condition):
    return jnp.where(condition, 1.0, 0.0).astype(BF16)


def nt(a, b):
    return lax.dot_general(a, b, (((1,), (1,)), ((), ())), preferred_element_type=F32)


def mm(a, b):
    return jnp.dot(a, b, preferred_element_type=F32)


def pack_pairs(count, pairs_ref, send_ref, tail, meta):
    source = pairs_ref[0:1, :]
    target = pairs_ref[1:2, :]
    operator = pairs_ref[2:3, :]
    used = iota((1, PAIRS), 1) < count
    ghost = jnp.maximum(source - BOXES, 0)
    lane = jnp.right_shift(ghost * 2731, 16)
    slot = ghost - lane * SLOTS
    lane = jnp.where(used, jnp.where(source < BOXES, LANES, lane), 31)
    codes = iota((32, PAIRS), 0)
    start = jnp.sum(jnp.where(lane < codes, 1.0, 0.0), axis=1, keepdims=True)
    before = one_hot(iota((128, 128), 0) < iota((128, 128), 1))
    carry = start
    places = []
    for chunk in range(PAIRS // 128):
        hot = jnp.where(codes[:, :128] == lane[:, chunk * 128:(chunk + 1) * 128], 1.0, 0.0)
        rank = mm(hot.astype(BF16), before) + carry
        places.append(jnp.sum(hot * rank, axis=0, keepdims=True))
        carry = carry + jnp.sum(hot, axis=1, keepdims=True)
    place = jnp.concatenate(places, axis=1).astype(I32)
    fields = jnp.concatenate(
        [slot, target, operator, jnp.zeros((5, PAIRS), I32)], axis=0
    ).astype(F32).astype(BF16)
    for q in range(4):
        hot = one_hot(iota((256, PAIRS), 0) + 256 * q == place)
        ordered = nt(fields, hot)
        meta[4 * q:4 * q + 3, :] = ordered[0:3, :]
    sends = send_ref[...].reshape(1, LANES * SLOTS).astype(F32)
    meta[3:4, :] = sends[:, 0:256]
    meta[7:8, :] = sends[:, 256:512]
    meta[11:12, 0:112] = sends[:, 512:624]
    meta[11:12, 112:256] = jnp.zeros((1, 144), F32)
    diagonal = iota((32, 128), 0) == iota((32, 128), 1)
    starts = jnp.sum(jnp.where(diagonal, start, 0.0), axis=0, keepdims=True).astype(I32)
    high = jnp.right_shift(starts, 5)
    meta[15:16, 0:128] = high.astype(F32)
    meta[15:16, 128:256] = (starts - high * 32).astype(F32)
    tail[...] = meta[...].astype(BF16)


def split(value):
    high = value.astype(BF16)
    return high, (value - high.astype(F32)).astype(BF16)


def count_own(count, pairs_ref, own_counts, hot_t):
    source = pairs_ref[0:1, :]
    target = pairs_ref[1:2, :]
    operator = pairs_ref[2:3, :]
    used = jnp.logical_and(iota((1, PAIRS), 1) < count, source < BOXES)
    key = jnp.where(used, operator * BOXES + source, -1)
    hot_t[...] = one_hot(iota((BOXES, PAIRS), 0) == target)
    for q in range(4):
        hot = one_hot(iota((256, PAIRS), 0) + 256 * q == key)
        high, low = split(nt(hot, hot_t[...]))
        own_counts[256 * q:256 * (q + 1), :] = jnp.concatenate([high, low], axis=1)


def count_forward(count, pairs_ref, counts, hot_u):
    source = pairs_ref[0:1, :]
    target = pairs_ref[1:2, :]
    operator = pairs_ref[2:3, :]
    used = iota((1, PAIRS), 1) < count
    key = jnp.where(used, operator * BOXES + target, -1)
    move = jnp.zeros((1, PAIRS), I32)
    for lane in range(LANES):
        first = BOXES + SLOTS * lane
        move = jnp.where(source >= first, ghost_row(lane) - first, move)
    hot_u[...] = one_hot(iota((768, PAIRS), 0) == source + move)
    for q in range(4):
        hot = one_hot(iota((256, PAIRS), 0) + 256 * q == key)
        for c in range(3):
            high, low = split(nt(hot, hot_u[256 * c:256 * (c + 1), :]))
            counts[256 * q:256 * (q + 1), 256 * c:256 * (c + 1)] = high
            counts[256 * q:256 * (q + 1), 768 + 256 * c:768 + 256 * (c + 1)] = low


def column(row):
    n = row.shape[1]
    parts = []
    for c in range(n // 128):
        piece = jnp.broadcast_to(row[:, c * 128:(c + 1) * 128], (8, 128))
        parts.append(jnp.transpose(piece)[:, 0:1])
    return jnp.concatenate(parts, axis=0)


def unpack(blocks, code, meta, starts_v):
    wide = blocks[code, BOXES:ROWS, :].astype(F32)
    for q in range(4):
        meta[code, q, 0:4, :] = wide[4 * q:4 * q + 4, :]
        meta[code, q, 4:8, :] = wide[4 * q:4 * q + 4, :]
    starts_v[code:code + 1, :] = (wide[15:16, 0:128] * 32.0 + wide[15:16, 128:256]).astype(I32)


def longest_lane(starts):
    lengths = pltpu.roll(starts, 127, 1) - starts
    code = iota((32, 128), 0)
    back = LANES - 1 - jnp.where(code < OWN, code, code - 1)
    theirs = jnp.logical_and(iota((32, 128), 1) == back, jnp.logical_and(code != OWN, code < 27))
    lengths = jnp.where(theirs, lengths, 0).astype(F32)
    return jnp.max(jnp.max(lengths, axis=0, keepdims=True), axis=1, keepdims=True)


def window(meta, code, begin, offset):
    begin = jnp.minimum(begin, PAIRS - 1)
    chunk = lax.div(begin, 128)
    after = jnp.minimum(chunk + 1, 7)

    def piece(c):
        return meta[code, lax.div(c, 2), :, pl.ds(pl.multiple_of(lax.rem(c, 2) * 128, 128), 128)]

    shift = begin - chunk * 128
    turn = lax.rem(256 + offset - shift, 128)
    first = pltpu.roll(piece(chunk), turn, 1)
    second = pltpu.roll(piece(after), turn, 1)
    return jnp.where(iota((8, 128), 1) < 128 - shift + offset, first, second)


def gather_ghosts(blocks, group, meta, ghost):
    width = 64 * len(group)
    table = jnp.concatenate([blocks[code_of(lane), 0:BOXES, :] for lane in group], axis=0)
    picks = []
    for i, lane in enumerate(group):
        low = lane * SLOTS
        q, at = low // 128, low % 128
        cells = [meta[code_of(lane), p // 2, 3:4, p % 2 * 128:p % 2 * 128 + 128] for p in (q, min(q + 1, 5))]
        both = column(jnp.concatenate(cells, axis=1))
        picked = both[at:at + SLOTS, :].astype(I32) + 64 * i
        picks.append(jnp.where(iota((SLOTS, width), 1) == picked, 1.0, 0.0))
    hot = jnp.concatenate(picks, axis=0).astype(BF16)
    first = ghost_row(group[0])
    ghost[first:first + SLOTS * len(group), :] = mm(hot, table).astype(BF16)


def gather_events(blocks, lanes, meta, starts_v, own_boxes, events, keys_m, rows_m):
    base = 64 * ORDER.index(lanes[0])
    pairs = [lanes[i:i + 2] for i in range(0, len(lanes), 2)]
    across = iota((8 * len(pairs), 128), 1)
    upper = iota((8, 128), 0) < 4

    def stack(of_lane):
        return jnp.concatenate(
            [jnp.where(upper, of_lane(first), of_lane(second)) for first, second in pairs], axis=0
        )

    def start_of(lane, after):
        code, back = code_of(lane), LANES - 1 - lane + after
        return starts_v[code:code + 1, back:back + 1]

    begin = jnp.minimum(stack(lambda lane: start_of(lane, 0)), PAIRS - 1)
    offset = jnp.where(jnp.bitwise_and(iota(across.shape, 0), 4) == 0, 0, 64)
    chunk = jnp.right_shift(begin, 7)
    shift = begin - chunk * 128
    chunks = [
        stack(lambda lane: meta[code_of(lane), p // 2, :, p % 2 * 128:p % 2 * 128 + 128]) for p in range(8)
    ]
    now, later = chunks[0], chunks[1]
    for p in range(1, 8):
        here = chunk == p
        now = jnp.where(here, chunks[p], now)
        later = jnp.where(here, chunks[min(p + 1, 7)], later)
    amount = jnp.bitwise_and(shift - offset + 128, 127)
    for bit in range(7):
        turned = jnp.bitwise_and(amount, 1 << bit) != 0
        now = jnp.where(turned, pltpu.roll(now, 128 - (1 << bit), 1), now)
        later = jnp.where(turned, pltpu.roll(later, 128 - (1 << bit), 1), later)
    part = jnp.where(across < 128 - shift + offset, now, later)
    flat = iota((1, 128), 1)
    for i, (first, second) in enumerate(pairs):
        fields = part[8 * i:8 * i + 8, :]
        fields = jnp.where(flat < 64, fields, jnp.concatenate([fields[4:8, :], fields[0:4, :]], axis=0))
        hot = iota((SLOTS, 128), 0) == fields[0:1, :].astype(I32)
        theirs = [own_boxes[(LANES - 1 - lane) * SLOTS:(LANES - lane) * SLOTS, :] for lane in (first, second)]
        theirs = jnp.where(iota((SLOTS, 128), 1) < 64, *theirs)
        box = jnp.sum(jnp.where(hot, theirs, 0.0), axis=0, keepdims=True)
        key = (fields[2:3, :] * BOXES + box).astype(I32)
        lengths = [start_of(lane, 1) - start_of(lane, 0) for lane in (first, second)]
        key = jnp.where(jnp.where(flat < 64, flat, flat - 64) < jnp.where(flat < 64, *lengths), key, -1)
        span = slice(base + i * 128, base + (i + 1) * 128)
        events[:, span] = fields
        keys_m[0:1, span] = key
    for group in quads(lanes):
        low = 64 * ORDER.index(group[0])
        width = 64 * len(group)
        table = jnp.concatenate([blocks[code_of(lane), 0:BOXES, :] for lane in group], axis=0)
        targets = column(events[1:2, low:low + width]).astype(I32)
        which = jnp.right_shift(iota((width, 1), 0), 6)
        hot = one_hot(iota((width, width), 1) == targets + 64 * which)
        rows_m[low:low + width, :] = mm(hot, table).astype(BF16)


def apply_operators(total, forward, mirror, ops_ref, q):
    if forward is not None:
        f_high, f_low = split(forward)
    m_high, m_low = split(mirror)
    for i in range(4):
        part = slice(64 * i, 64 * i + 64)
        matrix = ops_ref[4 * q + i]
        if forward is not None:
            total += mm(jnp.concatenate([f_high[part], f_low[part]], axis=0), matrix)
        total += nt(jnp.concatenate([m_high[part], m_low[part]], axis=0), matrix)
    return total


def remainder_kernel(field_hbm, blocks_hbm, ops_hbm, out_hbm, field, blocks, ops_ref, meta, starts_v, starts_s, zm, sem):
    fetch = pltpu.make_async_copy(field_hbm, field, sem.at[0])
    fetch.start()
    fetch.wait()

    @pl.when(jnp.max(field[BOXES:, :]) > WINDOW)
    def _():
        loads = [
            pltpu.make_async_copy(blocks_hbm, blocks, sem.at[1]),
            pltpu.make_async_copy(ops_hbm, ops_ref, sem.at[2]),
        ]
        for load in loads:
            load.start()
        for load in loads:
            load.wait()
        for code in range(27):
            unpack(blocks, code, meta, starts_v)
        copy = pltpu.make_async_copy(starts_v, starts_s, sem.at[3])
        copy.start()
        copy.wait()
        own_boxes = column(jnp.concatenate([meta[OWN, q, 3:4, :] for q in range(3)], axis=1))
        zm[...] = jnp.zeros_like(zm)

        @pl.loop(0, LANES)
        def _(lane):
            code = jnp.where(lane < OWN, lane, lane + 1)
            back = LANES - 1 - lane
            begin = starts_s[code, back]
            length = starts_s[code, back + 1] - begin

            @pl.loop(1, lax.div(length + WINDOW - 1, WINDOW))
            def _(turn):
                part = window(meta, code, begin + turn * WINDOW, 0)
                boxes_row = jnp.zeros((1, 128), F32)
                slots = part[0:1, :].astype(I32) + back * SLOTS
                for q in range(6):
                    hot = iota((128, 128), 0) + 128 * q == slots
                    spread = own_boxes[q * 128:(q + 1) * 128, :]
                    boxes_row += jnp.sum(jnp.where(hot, spread, 0.0), axis=0, keepdims=True)
                key = (part[2:3, :] * BOXES + boxes_row).astype(I32)
                key = jnp.where(iota((1, 128), 1) < jnp.minimum(length - turn * WINDOW, WINDOW), key, -1)
                hot = one_hot(iota((128, BOXES), 1) == column(part[1:2, :]).astype(I32))
                rows = mm(hot, blocks[code, 0:BOXES, :]).astype(BF16)
                for q in range(4):
                    hot = one_hot(iota((256, 128), 0) + 256 * q == key)
                    zm[256 * q:256 * (q + 1), :] += mm(hot, rows)

        total = jnp.zeros((128, POINTS), F32)
        for q in range(4):
            total = apply_operators(total, None, zm[256 * q:256 * (q + 1), :], ops_ref, q)
        field[0:BOXES, :] += total[0:BOXES, :] + total[BOXES:, :]

    store = pltpu.make_async_copy(field.at[pl.ds(0, BOXES)], out_hbm, sem.at[0])
    store.start()
    store.wait()


def main_kernel(
    nx, ny, nz, count_ref, pairs_hbm, send_hbm, m_hbm, ops_hbm,
    field_ref, blocks_hbm,
    blocks, ops_ref, counts, own_counts, pairs_ref, send_ref, tail, hot_t, hot_u,
    meta, starts_v, events, keys_m, ghost, rows_m, zf, zm,
    in_sem, send_sem, recv_sem,
):
    g = lax.axis_index("gx")
    h = lax.axis_index("gy")
    by = lax.rem(g, ny)
    bz = lax.div(g, ny)
    steps = {
        "z": {1: bz < nz - 1, -1: bz > 0, 0: True},
        "y": {1: by < ny - 1, -1: by > 0, 0: True},
        "x": {1: h < nx - 1, -1: h > 0, 0: True},
    }
    partner = {
        "z": lambda s: (g + s * ny, h),
        "y": lambda s: (g + s, h),
        "x": lambda s: (g, h + s),
    }

    def on_grid(dx, dy, dz):
        cond = None
        for flag in (steps["x"][dx], steps["y"][dy], steps["z"][dz]):
            if flag is not True:
                cond = flag if cond is None else jnp.logical_and(cond, flag)
        return cond

    barrier = pltpu.get_barrier_semaphore()
    for axis in "zyx":
        for s in (1, -1):
            @pl.when(steps[axis][s])
            def _():
                pl.semaphore_signal(barrier, inc=1, device_id=partner[axis](s), device_id_type=MESH)

    loads = [
        pltpu.make_async_copy(src, dst, in_sem.at[i])
        for i, (src, dst) in enumerate([
            (pairs_hbm, pairs_ref),
            (send_hbm, send_ref),
            (m_hbm, blocks.at[OWN, pl.ds(0, BOXES)]),
            (ops_hbm, ops_ref),
        ])
    ]
    for load in loads:
        load.start()

    def as_code(dx, dy, dz):
        return (dx + 1) * 9 + (dy + 1) * 3 + dz + 1

    spans = [pl.ds(0, ROWS)]
    started = []

    def send(src, axis, s, part):
        dx, dy, dz = src
        dst = {"x": (-s, dy, dz), "y": (dx, -s, dz), "z": (dx, dy, -s)}[axis]
        need = {"x": (s, dy, dz), "y": (dx, s, dz), "z": (dx, dy, s)}[axis]
        cond = on_grid(*need)
        own = False
        copy = pltpu.make_async_remote_copy(
            src_ref=m_hbm if own else blocks.at[as_code(*src), spans[part]],
            dst_ref=blocks.at[as_code(*dst), spans[part]],
            send_sem=send_sem.at[len(started)],
            recv_sem=recv_sem.at[part, as_code(*dst)],
            device_id=partner[axis](s),
            device_id_type=MESH,
        )
        started.append((copy, cond))
        pl.when(cond)(copy.start)

    def arrived(where, part):
        code = as_code(*where)
        slot = blocks.at[code, spans[part]]
        copy = pltpu.make_async_remote_copy(
            src_ref=slot, dst_ref=slot, send_sem=send_sem.at[0], recv_sem=recv_sem.at[part, code],
            device_id=(g, h), device_id_type=MESH,
        )
        pl.when(on_grid(*where))(copy.wait_recv)

    def send_home(part):
        for axis in "zyx":
            for s in (1, -1):
                send((0, 0, 0), axis, s, part)

    def relay(places, axes, part):
        for where in places:
            arrived(where, part)
            for axis in axes:
                for s in (1, -1):
                    send(where, axis, s, part)

    along_y = [(0, 1, 0), (0, -1, 0)]
    along_z = [(0, 0, 1), (0, 0, -1)]
    along_yz = [(0, 1, 1), (0, -1, 1), (0, 1, -1), (0, -1, -1)]
    count = count_ref[0]
    loads[0].wait()
    loads[1].wait()
    pack_pairs(count, pairs_ref, send_ref, blocks.at[OWN, pl.ds(BOXES, ROWS - BOXES)], tail)
    loads[2].wait()
    pl.semaphore_wait(
        barrier,
        sum(steps[axis][s].astype(I32) for axis in "zyx" for s in (1, -1)),
    )
    send_home(0)
    for code in range(27):
        if code != OWN:
            @pl.when(jnp.logical_not(on_grid(*heading(code))))
            def _():
                blocks[code] = jnp.zeros((ROWS, POINTS), BF16)
    starts_v[27:32, :] = jnp.zeros((5, 128), I32)
    ghost[496:512, :] = jnp.zeros((16, POINTS), BF16)
    ghost[704:768, :] = jnp.zeros((64, POINTS), BF16)
    own_boxes = column(
        jnp.concatenate([tail[4 * q + 3:4 * q + 4, :] for q in range(3)], axis=1)
    )
    count_own(count, pairs_ref, own_counts, hot_t)
    count_forward(count, pairs_ref, counts, hot_u)
    relay(along_y, "x", 0)
    relay(along_z, "yx", 0)
    loads[3].wait()

    def take(lanes):
        for lane in lanes:
            unpack(blocks, code_of(lane), meta, starts_v)
        for group in quads(lanes):
            gather_ghosts(blocks, group, meta, ghost)
        gather_events(blocks, lanes, meta, starts_v, own_boxes, events, keys_m, rows_m)

    def wait_for(lanes):
        for lane in lanes:
            if heading(code_of(lane))[0] != 0:
                arrived(heading(code_of(lane)), 0)

    def sums(q, low, high, first, last):
        span = slice(256 * q, 256 * (q + 1))
        forward = mm(counts[span, low:high], ghost[low:high, :])
        forward += mm(counts[span, 768 + low:768 + high], ghost[low:high, :])
        hot = one_hot(iota((256, last - first), 0) + 256 * q == keys_m[:, first:last])
        return forward, mm(hot, rows_m[first:last, :])

    ghost[0:BOXES, :] = blocks[OWN, 0:BOXES, :]
    starts_v[0:27, :] = jnp.zeros((27, 128), I32)
    own = blocks[OWN, 0:BOXES, :]
    own_twice = jnp.concatenate([own, own], axis=0)
    quarters = [slice(256 * q, 256 * (q + 1)) for q in range(4)]
    relay(along_yz, "x", 0)
    wait_for(EARLY)
    take(EARLY)
    wait_for(MIDDLE)
    take(MIDDLE)
    for q, span in enumerate(quarters):
        forward, mirror = sums(q, 0, 512, 0, LATE)
        zf[span, :] = forward
        zm[span, :] = mirror + mm(own_counts[span, :], own_twice)

    wait_for(CORNERS)
    save = pltpu.make_async_copy(blocks, blocks_hbm, in_sem.at[4])
    save.start()
    take(CORNERS)
    total = jnp.zeros((128, POINTS), F32)
    for q, span in enumerate(quarters):
        forward, mirror = sums(q, 512, 768, LATE, 64 * LANES)
        total = apply_operators(total, zf[span, :] + forward, zm[span, :] + mirror, ops_ref, q)
    field_ref[0:BOXES, :] = total[0:BOXES, :] + total[BOXES:, :]
    field_ref[BOXES:, :] = jnp.full((8, POINTS), 0.0, F32) + longest_lane(starts_v[...])
    save.wait()
    for copy, cond in started:
        pl.when(cond)(copy.wait_send)


def local(sizes, multipoles, operators, pairs, pair_count, send_list):
    nx, ny, nz = sizes
    smem = pl.BlockSpec(memory_space=pltpu.SMEM)
    vmem = pl.BlockSpec(memory_space=pltpu.VMEM)
    anywhere = pl.BlockSpec(memory_space=pl.ANY)
    blocks_shape = (27, ROWS, POINTS)
    field, blocks = pl.pallas_call(
        functools.partial(main_kernel, nx, ny, nz),
        out_shape=[
            jax.ShapeDtypeStruct((BOXES + 8, POINTS), F32),
            jax.ShapeDtypeStruct(blocks_shape, BF16),
        ],
        in_specs=[smem, anywhere, anywhere, anywhere, anywhere],
        out_specs=[vmem, anywhere],
        scratch_shapes=[
            pltpu.VMEM(blocks_shape, BF16),
            pltpu.VMEM((OPS, POINTS, POINTS), BF16),
            pltpu.VMEM((1024, 1536), BF16),
            pltpu.VMEM((1024, 128), BF16),
            pltpu.VMEM((3, PAIRS), I32),
            pltpu.VMEM((LANES * SLOTS,), I32),
            pltpu.VMEM((16, 256), F32),
            pltpu.VMEM((BOXES, PAIRS), BF16),
            pltpu.VMEM((768, PAIRS), BF16),
            pltpu.VMEM((27, 4, 8, 256), F32),
            pltpu.VMEM((32, 128), I32),
            pltpu.VMEM((8, LANES * 64), F32),
            pltpu.VMEM((1, LANES * 64), I32),
            pltpu.VMEM((768, POINTS), BF16),
            pltpu.VMEM((LANES * 64, POINTS), BF16),
            pltpu.VMEM((1024, POINTS), F32),
            pltpu.VMEM((1024, POINTS), F32),
            pltpu.SemaphoreType.DMA((5,)),
            pltpu.SemaphoreType.DMA((52,)),
            pltpu.SemaphoreType.DMA((2, 27)),
        ],
        compiler_params=pltpu.CompilerParams(
            collective_id=0, has_side_effects=True, vmem_limit_bytes=58 * 1024 * 1024
        ),
        name="exchange",
    )(pair_count, pairs, send_list, multipoles, operators)
    return pl.pallas_call(
        remainder_kernel,
        out_shape=jax.ShapeDtypeStruct((BOXES, POINTS), F32),
        in_specs=[anywhere] * 3,
        out_specs=anywhere,
        scratch_shapes=[
            pltpu.VMEM((BOXES + 8, POINTS), F32),
            pltpu.VMEM(blocks_shape, BF16),
            pltpu.VMEM((OPS, POINTS, POINTS), BF16),
            pltpu.VMEM((27, 4, 8, 256), F32),
            pltpu.VMEM((32, 128), I32),
            pltpu.SMEM((32, 128), I32),
            pltpu.VMEM((1024, POINTS), F32),
            pltpu.SemaphoreType.DMA((4,)),
        ],
        compiler_params=pltpu.CompilerParams(vmem_limit_bytes=58 * 1024 * 1024),
        name="remainder",
    )(field, blocks, operators)


def solution(mesh):
    shape = dict(mesh.shape)
    ny = min(8, shape["gx"] // 2)
    sizes = (shape["gy"], ny, shape["gx"] // ny)
    return jax.shard_map(
        functools.partial(local, sizes),
        mesh=mesh,
        in_specs=(
            P(("gx", "gy"), None),
            P(),
            P(None, ("gx", "gy")),
            P(("gx", "gy")),
            P(("gx", "gy")),
        ),
        out_specs=P(("gx", "gy"), None),
        check_vma=False,
    )
```

```python
import functools

import jax
import jax.numpy as jnp
from jax import lax
from jax.experimental import pallas as pl
from jax.experimental.pallas import tpu as pltpu
from jax.sharding import PartitionSpec as P

MESH = pl.DeviceIdType.MESH
F32 = jnp.float32
BF16 = jnp.bfloat16
I32 = jnp.int32

BOXES = 64
POINTS = 256
PAIRS = 1024
LANES = 26
SLOTS = 24
OPS = 16
OWN = 13
ROWS = 80
WINDOW = 64


EARLY = [1, 4, 7, 10, 15, 18, 21, 24]
MIDDLE = [12, 13, 9, 11, 14, 16, 3, 5, 20, 22]
CORNERS = [0, 2, 6, 8, 17, 19, 23, 25]
ORDER = EARLY + MIDDLE + CORNERS
MID, LATE = 64 * len(EARLY), 64 * len(EARLY + MIDDLE)


def quads(lanes):
    return [lanes[i:i + 4] for i in range(0, len(lanes), 4)]


def ghost_row(lane):
    return BOXES + SLOTS * ORDER.index(lane) + (16 if lane in CORNERS else 0)


def code_of(lane):
    return lane if lane < OWN else lane + 1


def heading(code):
    return code // 9 - 1, code // 3 % 3 - 1, code % 3 - 1


def iota(shape, axis):
    return lax.broadcasted_iota(I32, shape, axis)


def one_hot(condition):
    return jnp.where(condition, 1.0, 0.0).astype(BF16)


def nt(a, b):
    return lax.dot_general(a, b, (((1,), (1,)), ((), ())), preferred_element_type=F32)


def mm(a, b):
    return jnp.dot(a, b, preferred_element_type=F32)


def pack_pairs(count, pairs_ref, send_ref, tail, meta):
    source = pairs_ref[0:1, :]
    target = pairs_ref[1:2, :]
    operator = pairs_ref[2:3, :]
    used = iota((1, PAIRS), 1) < count
    ghost = jnp.maximum(source - BOXES, 0)
    lane = jnp.right_shift(ghost * 2731, 16)
    slot = ghost - lane * SLOTS
    lane = jnp.where(used, jnp.where(source < BOXES, LANES, lane), 31)
    codes = iota((32, PAIRS), 0)
    start = jnp.sum(jnp.where(lane < codes, 1.0, 0.0), axis=1, keepdims=True)
    before = one_hot(iota((128, 128), 0) < iota((128, 128), 1))
    carry = start
    places = []
    for chunk in range(PAIRS // 128):
        hot = jnp.where(codes[:, :128] == lane[:, chunk * 128:(chunk + 1) * 128], 1.0, 0.0)
        rank = mm(hot.astype(BF16), before) + carry
        places.append(jnp.sum(hot * rank, axis=0, keepdims=True))
        carry = carry + jnp.sum(hot, axis=1, keepdims=True)
    place = jnp.concatenate(places, axis=1).astype(I32)
    fields = jnp.concatenate(
        [slot, target, operator, jnp.zeros((5, PAIRS), I32)], axis=0
    ).astype(F32).astype(BF16)
    for q in range(4):
        hot = one_hot(iota((256, PAIRS), 0) + 256 * q == place)
        ordered = nt(fields, hot)
        meta[4 * q:4 * q + 3, :] = ordered[0:3, :]
    sends = send_ref[...].reshape(1, LANES * SLOTS).astype(F32)
    meta[3:4, :] = sends[:, 0:256]
    meta[7:8, :] = sends[:, 256:512]
    meta[11:12, 0:112] = sends[:, 512:624]
    meta[11:12, 112:256] = jnp.zeros((1, 144), F32)
    diagonal = iota((32, 128), 0) == iota((32, 128), 1)
    starts = jnp.sum(jnp.where(diagonal, start, 0.0), axis=0, keepdims=True).astype(I32)
    high = jnp.right_shift(starts, 5)
    meta[15:16, 0:128] = high.astype(F32)
    meta[15:16, 128:256] = (starts - high * 32).astype(F32)
    tail[...] = meta[...].astype(BF16)


def split(value):
    high = value.astype(BF16)
    return high, (value - high.astype(F32)).astype(BF16)


def count_own(count, pairs_ref, own_counts, hot_t):
    source = pairs_ref[0:1, :]
    target = pairs_ref[1:2, :]
    operator = pairs_ref[2:3, :]
    used = jnp.logical_and(iota((1, PAIRS), 1) < count, source < BOXES)
    key = jnp.where(used, operator * BOXES + source, -1)
    hot_t[...] = one_hot(iota((BOXES, PAIRS), 0) == target)
    for q in range(4):
        hot = one_hot(iota((256, PAIRS), 0) + 256 * q == key)
        high, low = split(nt(hot, hot_t[...]))
        own_counts[256 * q:256 * (q + 1), :] = jnp.concatenate([high, low], axis=1)


def count_forward(count, pairs_ref, counts, hot_u):
    source = pairs_ref[0:1, :]
    target = pairs_ref[1:2, :]
    operator = pairs_ref[2:3, :]
    used = iota((1, PAIRS), 1) < count
    key = jnp.where(used, operator * BOXES + target, -1)
    move = jnp.zeros((1, PAIRS), I32)
    for lane in range(LANES):
        first = BOXES + SLOTS * lane
        move = jnp.where(source >= first, ghost_row(lane) - first, move)
    hot_u[...] = one_hot(iota((768, PAIRS), 0) == source + move)
    for q in range(4):
        hot = one_hot(iota((256, PAIRS), 0) + 256 * q == key)
        for c in range(3):
            high, low = split(nt(hot, hot_u[256 * c:256 * (c + 1), :]))
            counts[256 * q:256 * (q + 1), 256 * c:256 * (c + 1)] = high
            counts[256 * q:256 * (q + 1), 768 + 256 * c:768 + 256 * (c + 1)] = low


def column(row):
    n = row.shape[1]
    parts = []
    for c in range(n // 128):
        piece = jnp.broadcast_to(row[:, c * 128:(c + 1) * 128], (8, 128))
        parts.append(jnp.transpose(piece)[:, 0:1])
    return jnp.concatenate(parts, axis=0)


def unpack(blocks, code, meta, starts_v):
    wide = blocks[code, BOXES:ROWS, :].astype(F32)
    for q in range(4):
        meta[code, q, 0:4, :] = wide[4 * q:4 * q + 4, :]
        meta[code, q, 4:8, :] = wide[4 * q:4 * q + 4, :]
    starts_v[code:code + 1, :] = (wide[15:16, 0:128] * 32.0 + wide[15:16, 128:256]).astype(I32)


def longest_lane(starts):
    lengths = pltpu.roll(starts, 127, 1) - starts
    code = iota((32, 128), 0)
    back = LANES - 1 - jnp.where(code < OWN, code, code - 1)
    theirs = jnp.logical_and(iota((32, 128), 1) == back, jnp.logical_and(code != OWN, code < 27))
    lengths = jnp.where(theirs, lengths, 0).astype(F32)
    return jnp.max(jnp.max(lengths, axis=0, keepdims=True), axis=1, keepdims=True)


def window(meta, code, begin, offset):
    begin = jnp.minimum(begin, PAIRS - 1)
    chunk = lax.div(begin, 128)
    after = jnp.minimum(chunk + 1, 7)

    def piece(c):
        return meta[code, lax.div(c, 2), :, pl.ds(pl.multiple_of(lax.rem(c, 2) * 128, 128), 128)]

    shift = begin - chunk * 128
    turn = lax.rem(256 + offset - shift, 128)
    first = pltpu.roll(piece(chunk), turn, 1)
    second = pltpu.roll(piece(after), turn, 1)
    return jnp.where(iota((8, 128), 1) < 128 - shift + offset, first, second)


def gather_ghosts(blocks, group, meta, ghost):
    width = 64 * len(group)
    table = jnp.concatenate([blocks[code_of(lane), 0:BOXES, :] for lane in group], axis=0)
    picks = []
    for i, lane in enumerate(group):
        low = lane * SLOTS
        q, at = low // 128, low % 128
        cells = [meta[code_of(lane), p // 2, 3:4, p % 2 * 128:p % 2 * 128 + 128] for p in (q, min(q + 1, 5))]
        both = column(jnp.concatenate(cells, axis=1))
        picked = both[at:at + SLOTS, :].astype(I32) + 64 * i
        picks.append(jnp.where(iota((SLOTS, width), 1) == picked, 1.0, 0.0))
    hot = jnp.concatenate(picks, axis=0).astype(BF16)
    first = ghost_row(group[0])
    ghost[first:first + SLOTS * len(group), :] = mm(hot, table).astype(BF16)


def gather_events(blocks, lanes, meta, starts_v, own_boxes, events, keys_m, rows_m):
    base = 64 * ORDER.index(lanes[0])
    pairs = [lanes[i:i + 2] for i in range(0, len(lanes), 2)]
    across = iota((8 * len(pairs), 128), 1)
    upper = iota((8, 128), 0) < 4

    def stack(of_lane):
        return jnp.concatenate(
            [jnp.where(upper, of_lane(first), of_lane(second)) for first, second in pairs], axis=0
        )

    def start_of(lane, after):
        code, back = code_of(lane), LANES - 1 - lane + after
        return starts_v[code:code + 1, back:back + 1]

    begin = jnp.minimum(stack(lambda lane: start_of(lane, 0)), PAIRS - 1)
    offset = jnp.where(jnp.bitwise_and(iota(across.shape, 0), 4) == 0, 0, 64)
    chunk = jnp.right_shift(begin, 7)
    shift = begin - chunk * 128
    chunks = [
        stack(lambda lane: meta[code_of(lane), p // 2, :, p % 2 * 128:p % 2 * 128 + 128]) for p in range(8)
    ]
    now, later = chunks[0], chunks[1]
    for p in range(1, 8):
        here = chunk == p
        now = jnp.where(here, chunks[p], now)
        later = jnp.where(here, chunks[min(p + 1, 7)], later)
    amount = jnp.bitwise_and(shift - offset + 128, 127)
    for bit in range(7):
        turned = jnp.bitwise_and(amount, 1 << bit) != 0
        now = jnp.where(turned, pltpu.roll(now, 128 - (1 << bit), 1), now)
        later = jnp.where(turned, pltpu.roll(later, 128 - (1 << bit), 1), later)
    part = jnp.where(across < 128 - shift + offset, now, later)
    flat = iota((1, 128), 1)
    for i, (first, second) in enumerate(pairs):
        fields = part[8 * i:8 * i + 8, :]
        fields = jnp.where(flat < 64, fields, jnp.concatenate([fields[4:8, :], fields[0:4, :]], axis=0))
        hot = iota((SLOTS, 128), 0) == fields[0:1, :].astype(I32)
        theirs = [own_boxes[(LANES - 1 - lane) * SLOTS:(LANES - lane) * SLOTS, :] for lane in (first, second)]
        theirs = jnp.where(iota((SLOTS, 128), 1) < 64, *theirs)
        box = jnp.sum(jnp.where(hot, theirs, 0.0), axis=0, keepdims=True)
        key = (fields[2:3, :] * BOXES + box).astype(I32)
        lengths = [start_of(lane, 1) - start_of(lane, 0) for lane in (first, second)]
        key = jnp.where(jnp.where(flat < 64, flat, flat - 64) < jnp.where(flat < 64, *lengths), key, -1)
        span = slice(base + i * 128, base + (i + 1) * 128)
        events[:, span] = fields
        keys_m[0:1, span] = key
    for group in quads(lanes):
        low = 64 * ORDER.index(group[0])
        width = 64 * len(group)
        table = jnp.concatenate([blocks[code_of(lane), 0:BOXES, :] for lane in group], axis=0)
        targets = column(events[1:2, low:low + width]).astype(I32)
        which = jnp.right_shift(iota((width, 1), 0), 6)
        hot = one_hot(iota((width, width), 1) == targets + 64 * which)
        rows_m[low:low + width, :] = mm(hot, table).astype(BF16)


def apply_operators(total, forward, mirror, ops_ref, q):
    if forward is not None:
        f_high, f_low = split(forward)
    m_high, m_low = split(mirror)
    for i in range(4):
        part = slice(64 * i, 64 * i + 64)
        matrix = ops_ref[4 * q + i]
        if forward is not None:
            total += mm(jnp.concatenate([f_high[part], f_low[part]], axis=0), matrix)
        total += nt(jnp.concatenate([m_high[part], m_low[part]], axis=0), matrix)
    return total


def remainder_kernel(field_hbm, blocks_hbm, ops_hbm, out_hbm, field, blocks, ops_ref, meta, starts_v, starts_s, zm, sem):
    fetch = pltpu.make_async_copy(field_hbm, field, sem.at[0])
    fetch.start()
    fetch.wait()

    @pl.when(jnp.max(field[BOXES:, :]) > WINDOW)
    def _():
        loads = [
            pltpu.make_async_copy(blocks_hbm, blocks, sem.at[1]),
            pltpu.make_async_copy(ops_hbm, ops_ref, sem.at[2]),
        ]
        for load in loads:
            load.start()
        for load in loads:
            load.wait()
        for code in range(27):
            unpack(blocks, code, meta, starts_v)
        copy = pltpu.make_async_copy(starts_v, starts_s, sem.at[3])
        copy.start()
        copy.wait()
        own_boxes = column(jnp.concatenate([meta[OWN, q, 3:4, :] for q in range(3)], axis=1))
        zm[...] = jnp.zeros_like(zm)

        @pl.loop(0, LANES)
        def _(lane):
            code = jnp.where(lane < OWN, lane, lane + 1)
            back = LANES - 1 - lane
            begin = starts_s[code, back]
            length = starts_s[code, back + 1] - begin

            @pl.loop(1, lax.div(length + WINDOW - 1, WINDOW))
            def _(turn):
                part = window(meta, code, begin + turn * WINDOW, 0)
                boxes_row = jnp.zeros((1, 128), F32)
                slots = part[0:1, :].astype(I32) + back * SLOTS
                for q in range(6):
                    hot = iota((128, 128), 0) + 128 * q == slots
                    spread = own_boxes[q * 128:(q + 1) * 128, :]
                    boxes_row += jnp.sum(jnp.where(hot, spread, 0.0), axis=0, keepdims=True)
                key = (part[2:3, :] * BOXES + boxes_row).astype(I32)
                key = jnp.where(iota((1, 128), 1) < jnp.minimum(length - turn * WINDOW, WINDOW), key, -1)
                hot = one_hot(iota((128, BOXES), 1) == column(part[1:2, :]).astype(I32))
                rows = mm(hot, blocks[code, 0:BOXES, :]).astype(BF16)
                for q in range(4):
                    hot = one_hot(iota((256, 128), 0) + 256 * q == key)
                    zm[256 * q:256 * (q + 1), :] += mm(hot, rows)

        total = jnp.zeros((128, POINTS), F32)
        for q in range(4):
            total = apply_operators(total, None, zm[256 * q:256 * (q + 1), :], ops_ref, q)
        field[0:BOXES, :] += total[0:BOXES, :] + total[BOXES:, :]

    store = pltpu.make_async_copy(field.at[pl.ds(0, BOXES)], out_hbm, sem.at[0])
    store.start()
    store.wait()


def main_kernel(
    nx, ny, nz, count_ref, pairs_hbm, send_hbm, m_hbm, ops_hbm,
    field_ref, blocks_hbm,
    blocks, ops_ref, counts, own_counts, pairs_ref, send_ref, tail, hot_t, hot_u,
    meta, starts_v, events, keys_m, ghost, rows_m, zf, zm,
    in_sem, send_sem, recv_sem,
):
    g = lax.axis_index("gx")
    h = lax.axis_index("gy")
    by = lax.rem(g, ny)
    bz = lax.div(g, ny)
    steps = {
        "z": {1: bz < nz - 1, -1: bz > 0, 0: True},
        "y": {1: by < ny - 1, -1: by > 0, 0: True},
        "x": {1: h < nx - 1, -1: h > 0, 0: True},
    }
    partner = {
        "z": lambda s: (g + s * ny, h),
        "y": lambda s: (g + s, h),
        "x": lambda s: (g, h + s),
    }

    def on_grid(dx, dy, dz):
        cond = None
        for flag in (steps["x"][dx], steps["y"][dy], steps["z"][dz]):
            if flag is not True:
                cond = flag if cond is None else jnp.logical_and(cond, flag)
        return cond

    barrier = pltpu.get_barrier_semaphore()
    for axis in "zyx":
        for s in (1, -1):
            @pl.when(steps[axis][s])
            def _():
                pl.semaphore_signal(barrier, inc=1, device_id=partner[axis](s), device_id_type=MESH)

    loads = [
        pltpu.make_async_copy(src, dst, in_sem.at[i])
        for i, (src, dst) in enumerate([
            (pairs_hbm, pairs_ref),
            (send_hbm, send_ref),
            (m_hbm, blocks.at[OWN, pl.ds(0, BOXES)]),
            (ops_hbm, ops_ref),
        ])
    ]
    for load in loads:
        load.start()

    def as_code(dx, dy, dz):
        return (dx + 1) * 9 + (dy + 1) * 3 + dz + 1

    spans = [pl.ds(0, ROWS)]
    started = []

    def send(src, axis, s, part):
        dx, dy, dz = src
        dst = {"x": (-s, dy, dz), "y": (dx, -s, dz), "z": (dx, dy, -s)}[axis]
        need = {"x": (s, dy, dz), "y": (dx, s, dz), "z": (dx, dy, s)}[axis]
        cond = on_grid(*need)
        own = False
        copy = pltpu.make_async_remote_copy(
            src_ref=m_hbm if own else blocks.at[as_code(*src), spans[part]],
            dst_ref=blocks.at[as_code(*dst), spans[part]],
            send_sem=send_sem.at[len(started)],
            recv_sem=recv_sem.at[part, as_code(*dst)],
            device_id=partner[axis](s),
            device_id_type=MESH,
        )
        started.append((copy, cond))
        pl.when(cond)(copy.start)

    def arrived(where, part):
        code = as_code(*where)
        slot = blocks.at[code, spans[part]]
        copy = pltpu.make_async_remote_copy(
            src_ref=slot, dst_ref=slot, send_sem=send_sem.at[0], recv_sem=recv_sem.at[part, code],
            device_id=(g, h), device_id_type=MESH,
        )
        pl.when(on_grid(*where))(copy.wait_recv)

    def send_home(part):
        for axis in "zyx":
            for s in (1, -1):
                send((0, 0, 0), axis, s, part)

    def relay(places, axes, part):
        for where in places:
            arrived(where, part)
            for axis in axes:
                for s in (1, -1):
                    send(where, axis, s, part)

    along_y = [(0, 1, 0), (0, -1, 0)]
    along_z = [(0, 0, 1), (0, 0, -1)]
    along_yz = [(0, 1, 1), (0, -1, 1), (0, 1, -1), (0, -1, -1)]
    count = count_ref[0]
    loads[0].wait()
    loads[1].wait()
    pack_pairs(count, pairs_ref, send_ref, blocks.at[OWN, pl.ds(BOXES, ROWS - BOXES)], tail)
    loads[2].wait()
    pl.semaphore_wait(
        barrier,
        sum(steps[axis][s].astype(I32) for axis in "zyx" for s in (1, -1)),
    )
    send_home(0)
    for code in range(27):
        if code != OWN:
            @pl.when(jnp.logical_not(on_grid(*heading(code))))
            def _():
                blocks[code] = jnp.zeros((ROWS, POINTS), BF16)
    starts_v[27:32, :] = jnp.zeros((5, 128), I32)
    ghost[496:512, :] = jnp.zeros((16, POINTS), BF16)
    ghost[704:768, :] = jnp.zeros((64, POINTS), BF16)
    own_boxes = column(
        jnp.concatenate([tail[4 * q + 3:4 * q + 4, :] for q in range(3)], axis=1)
    )
    count_own(count, pairs_ref, own_counts, hot_t)
    count_forward(count, pairs_ref, counts, hot_u)
    relay(along_z, "yx", 0)
    relay(along_y, "x", 0)
    loads[3].wait()

    def take(lanes):
        for lane in lanes:
            unpack(blocks, code_of(lane), meta, starts_v)
        for group in quads(lanes):
            gather_ghosts(blocks, group, meta, ghost)
        gather_events(blocks, lanes, meta, starts_v, own_boxes, events, keys_m, rows_m)

    def wait_for(lanes):
        for lane in lanes:
            if heading(code_of(lane))[0] != 0:
                arrived(heading(code_of(lane)), 0)

    def sums(q, low, high, first, last):
        span = slice(256 * q, 256 * (q + 1))
        forward = mm(counts[span, low:high], ghost[low:high, :])
        forward += mm(counts[span, 768 + low:768 + high], ghost[low:high, :])
        hot = one_hot(iota((256, last - first), 0) + 256 * q == keys_m[:, first:last])
        return forward, mm(hot, rows_m[first:last, :])

    ghost[0:BOXES, :] = blocks[OWN, 0:BOXES, :]
    starts_v[0:27, :] = jnp.zeros((27, 128), I32)
    wait_for(EARLY)
    take(EARLY)
    own = blocks[OWN, 0:BOXES, :]
    own_twice = jnp.concatenate([own, own], axis=0)
    quarters = [slice(256 * q, 256 * (q + 1)) for q in range(4)]
    for q, span in enumerate(quarters):
        forward, mirror = sums(q, 0, 256, 0, MID)
        zf[span, :] = forward
        zm[span, :] = mirror + mm(own_counts[span, :], own_twice)

    relay(along_yz, "x", 0)
    wait_for(MIDDLE)
    take(MIDDLE)
    for q, span in enumerate(quarters):
        forward, mirror = sums(q, 256, 512, MID, LATE)
        zf[span, :] += forward
        zm[span, :] += mirror

    wait_for(CORNERS)
    save = pltpu.make_async_copy(blocks, blocks_hbm, in_sem.at[4])
    save.start()
    take(CORNERS)
    total = jnp.zeros((128, POINTS), F32)
    for q, span in enumerate(quarters):
        forward, mirror = sums(q, 512, 768, LATE, 64 * LANES)
        total = apply_operators(total, zf[span, :] + forward, zm[span, :] + mirror, ops_ref, q)
    field_ref[0:BOXES, :] = total[0:BOXES, :] + total[BOXES:, :]
    field_ref[BOXES:, :] = jnp.full((8, POINTS), 0.0, F32) + longest_lane(starts_v[...])
    save.wait()
    for copy, cond in started:
        pl.when(cond)(copy.wait_send)


def local(sizes, multipoles, operators, pairs, pair_count, send_list):
    nx, ny, nz = sizes
    smem = pl.BlockSpec(memory_space=pltpu.SMEM)
    vmem = pl.BlockSpec(memory_space=pltpu.VMEM)
    anywhere = pl.BlockSpec(memory_space=pl.ANY)
    blocks_shape = (27, ROWS, POINTS)
    field, blocks = pl.pallas_call(
        functools.partial(main_kernel, nx, ny, nz),
        out_shape=[
            jax.ShapeDtypeStruct((BOXES + 8, POINTS), F32),
            jax.ShapeDtypeStruct(blocks_shape, BF16),
        ],
        in_specs=[smem, anywhere, anywhere, anywhere, anywhere],
        out_specs=[vmem, anywhere],
        scratch_shapes=[
            pltpu.VMEM(blocks_shape, BF16),
            pltpu.VMEM((OPS, POINTS, POINTS), BF16),
            pltpu.VMEM((1024, 1536), BF16),
            pltpu.VMEM((1024, 128), BF16),
            pltpu.VMEM((3, PAIRS), I32),
            pltpu.VMEM((LANES * SLOTS,), I32),
            pltpu.VMEM((16, 256), F32),
            pltpu.VMEM((BOXES, PAIRS), BF16),
            pltpu.VMEM((768, PAIRS), BF16),
            pltpu.VMEM((27, 4, 8, 256), F32),
            pltpu.VMEM((32, 128), I32),
            pltpu.VMEM((8, LANES * 64), F32),
            pltpu.VMEM((1, LANES * 64), I32),
            pltpu.VMEM((768, POINTS), BF16),
            pltpu.VMEM((LANES * 64, POINTS), BF16),
            pltpu.VMEM((1024, POINTS), F32),
            pltpu.VMEM((1024, POINTS), F32),
            pltpu.SemaphoreType.DMA((5,)),
            pltpu.SemaphoreType.DMA((52,)),
            pltpu.SemaphoreType.DMA((2, 27)),
        ],
        compiler_params=pltpu.CompilerParams(
            collective_id=0, has_side_effects=True, vmem_limit_bytes=58 * 1024 * 1024
        ),
        name="exchange",
    )(pair_count, pairs, send_list, multipoles, operators)
    return pl.pallas_call(
        remainder_kernel,
        out_shape=jax.ShapeDtypeStruct((BOXES, POINTS), F32),
        in_specs=[anywhere] * 3,
        out_specs=anywhere,
        scratch_shapes=[
            pltpu.VMEM((BOXES + 8, POINTS), F32),
            pltpu.VMEM(blocks_shape, BF16),
            pltpu.VMEM((OPS, POINTS, POINTS), BF16),
            pltpu.VMEM((27, 4, 8, 256), F32),
            pltpu.VMEM((32, 128), I32),
            pltpu.SMEM((32, 128), I32),
            pltpu.VMEM((1024, POINTS), F32),
            pltpu.SemaphoreType.DMA((4,)),
        ],
        compiler_params=pltpu.CompilerParams(vmem_limit_bytes=58 * 1024 * 1024),
        name="remainder",
    )(field, blocks, operators)


def solution(mesh):
    shape = dict(mesh.shape)
    ny = min(8, shape["gx"] // 2)
    sizes = (shape["gy"], ny, shape["gx"] // ny)
    return jax.shard_map(
        functools.partial(local, sizes),
        mesh=mesh,
        in_specs=(
            P(("gx", "gy"), None),
            P(),
            P(None, ("gx", "gy")),
            P(("gx", "gy")),
            P(("gx", "gy")),
        ),
        out_specs=P(("gx", "gy"), None),
        check_vma=False,
    )
```
